256 devices in a mesh: ctx: 32 (over x, z), head: 8 (over y, core).
Axes of the slice: x: 4, y: 4, z: 8, core: 2. Of those that a mesh axis runs over, the one named last changes fastest.
Arguments:
- latents: bfloat16 [2048, 1024], P('ctx'), may hold values from -4 to 4
- frames: bfloat16 [65536, 1024], P(('ctx', 'head')), may hold values from -200 to 200
- block_lists: int32 [16, 256], replicated, may hold values from 0 to 511, as said below
- query_weight: bfloat16 [1024, 1024], P(None, 'head')
- key_weight: bfloat16 [1024, 1024], replicated
- value_weight: bfloat16 [1024, 1024], replicated, may hold values from -0.1875 to 0.1875
- output_weight: bfloat16 [1024, 1024], P('head'), may hold values from -0.1875 to 0.1875
Outputs:
- mixed: bfloat16 [2048, 1024], P(('ctx', 'head'))
The draws below stay inside these ranges and needn't reach their ends.
Inputs may be any that keep to these rules, and one draw needn't show every extreme that they name: `block_lists`: each row lists 256 different frame blocks in rising order; frame blocks 0 and 511 appear in every row.
All inputs are finite; a program needn't handle non-finite values.
Results may differ from the reference program's by a relative error of at most 0.02.
Values may be sent and summed in bfloat16 or wider, within the bound.
A program may use at most 128 MiB of HBM per device.

```python
import jax
import jax.numpy as jnp
from jax import lax

H = 16
HS = 64
D = 1024
NL = 2048
BLK = 128
FRAMES = 65536
FB = 512
NLB = 16


def shared_latents(key):
    latent_key = jax.random.fold_in(key, 101)
    return jnp.clip(jax.random.normal(latent_key, (NL, D), jnp.float32), -4.0, 4.0)


def shared_lists(key):
    list_key = jax.random.fold_in(key, 102)
    block_count = FRAMES // BLK
    random_part = jax.random.randint(list_key, (NL // BLK, block_count), 0, 2 ** 17)
    block_ids = jnp.arange(block_count, dtype=jnp.int32)
    rising = block_ids * 2 ** 17 // block_count
    forced = jnp.where((block_ids == 0) | (block_ids == block_count - 1), 2 ** 18, 0)
    ranking = (random_part + rising[None, :] + forced[None, :]) * block_count + block_ids[None, :]
    chosen = lax.top_k(ranking, block_count // 2)[1]
    return jnp.sort(chosen, axis=1).astype(jnp.int32)


def shared_query(key):
    query_key = jax.random.fold_in(key, 103)
    return jax.random.normal(query_key, (D, D), jnp.float32) * D ** (-0.5)


def draw_latents(key, part):
    return shared_latents(key).astype(jnp.bfloat16)


def draw_block_lists(key, part):
    return shared_lists(key)


def draw_query_weight(key, part):
    return shared_query(key).astype(jnp.bfloat16)


def draw_key_weight(key, part):
    key = jax.random.fold_in(key, 4)
    own_part = jax.random.normal(key, (D, D), jnp.float32) * D ** (-0.5)
    return own_part.astype(jnp.bfloat16)


def draw_frames(key, part):
    key = jax.random.fold_in(key, 5)
    return jnp.clip(jax.random.normal(key, (FRAMES, D), jnp.float32) * 2.5, -15.0, 15.0).astype(jnp.bfloat16)


def shard_levels(stream_key, extent, shards, low, top_value):
    loudness = 1.0
    for position, blocks in shards:
        steps = jax.random.uniform(jax.random.fold_in(jax.random.fold_in(stream_key, 6), position), (blocks,), jnp.float32, low / len(shards), top_value / len(shards))
        loudness = loudness * jnp.repeat(jnp.exp(steps), extent[position] // blocks).reshape((-1,) + (1,) * (len(extent) - 1 - position))
    return loudness


def bell_draw(own_key, shape, width, most, cuts=(), kind=jnp.bfloat16):
    entries = width * jax.random.normal(own_key, shape, jnp.float32)
    if cuts:
        entries = entries * shard_levels(own_key, shape, cuts, -0.22, 0.18)
    return jnp.clip(entries, -most, most).astype(kind)


def setup_inputs(seed: int = 0) -> dict:
    key_of = jax.random.split(jax.random.key(seed), 8)
    latents = draw_latents(jax.random.fold_in(key_of[7], 71), 0)
    frames = draw_frames(jax.random.fold_in(key_of[7], 71), 0)
    block_lists = draw_block_lists(jax.random.fold_in(key_of[7], 71), 0)
    query_weight = draw_query_weight(jax.random.fold_in(key_of[7], 71), 0)
    key_weight = draw_key_weight(jax.random.fold_in(key_of[7], 71), 0)
    value_weight = bell_draw(key_of[5], (D, D), D ** -0.5, 0.1875)
    output_weight = bell_draw(key_of[6], (D, D), D ** -0.5, 0.1875, ((0, 8),))
    return dict(latents=latents, frames=frames, block_lists=block_lists, query_weight=query_weight, key_weight=key_weight, value_weight=value_weight, output_weight=output_weight)


NEG_FILL = -1.0e30


def reference(latents, frames, block_lists, query_weight, key_weight, value_weight, output_weight):
    scale_factor = HS ** -0.5
    queries = jnp.dot(latents, query_weight, preferred_element_type=jnp.float32).astype(jnp.bfloat16)
    key_rows = jnp.dot(frames, key_weight, preferred_element_type=jnp.float32).astype(jnp.bfloat16)
    value_rows = jnp.dot(frames, value_weight, preferred_element_type=jnp.float32).astype(jnp.bfloat16)
    frame_ids = jnp.arange(FB, dtype=jnp.int32)
    visible = jnp.any(block_lists[:, :, None] == frame_ids[None, None, :], axis=1)
    query_heads = queries.reshape(NLB, BLK, H, HS).transpose(2, 0, 1, 3)
    key_heads = key_rows.reshape(FRAMES, H, HS).transpose(1, 0, 2)
    value_heads = value_rows.reshape(FRAMES, H, HS).transpose(1, 0, 2)

    def one_head(operands):
        head_queries, head_keys, head_values = operands

        def one_block(block_operands):
            block_queries, block_visible = block_operands
            scores = jnp.dot(block_queries, head_keys.T, preferred_element_type=jnp.float32) * scale_factor
            allowed = jnp.repeat(block_visible, BLK)[None, :]
            scores = jnp.where(allowed, scores, NEG_FILL)
            row_max = jnp.max(scores, axis=1, keepdims=True)
            exponent = jnp.where(allowed, jnp.exp(scores - row_max), 0.0)
            totals = jnp.sum(exponent, axis=1, keepdims=True)
            weighted = jnp.dot(exponent.astype(jnp.bfloat16), head_values, preferred_element_type=jnp.float32)
            return weighted / totals

        return lax.map(one_block, (head_queries, visible))

    attended = lax.map(one_head, (query_heads, key_heads, value_heads))
    attended = attended.transpose(1, 2, 0, 3).reshape(NL, D).astype(jnp.bfloat16)
    return jnp.dot(attended, output_weight, preferred_element_type=jnp.float32).astype(jnp.bfloat16)
```

```python
import functools

import jax
import jax.numpy as jnp
from jax import lax
from jax.experimental import pallas as pl
from jax.experimental.pallas import tpu as pltpu
from jax.sharding import PartitionSpec as P

HS = 64
BLK = 128
LANES = 2 * HS
PACK = HS + 16
SCALE = HS ** (-0.5) * 1.4426950408889634
NEG = -1e30
MESH = pl.DeviceIdType.MESH
F32, BF16 = jnp.float32, jnp.bfloat16


def near_first(count):
    return sorted(range(count), key=lambda step: (min(step, count - step), step))


def far_first(count):
    return [step for step in near_first(count)[::-1] if step]


def split_parts(value, count):
    parts = []
    for _ in range(count):
        part = value.astype(BF16).astype(F32)
        parts.append(part)
        value = value - part
    return parts


def pack_stats(top, total):
    rows = split_parts(total, 2) + split_parts(top, 3)
    row_id = lax.broadcasted_iota(jnp.int32, (16, top.shape[1]), 0)
    out = jnp.zeros((16, top.shape[1]), F32)
    for index, row in enumerate(rows):
        out = jnp.where(row_id == index, jnp.broadcast_to(row, out.shape), out)
    return out.astype(BF16)


def unpack_stats(stats):
    stats = stats.astype(F32)
    return stats[2:3] + stats[3:4] + stats[4:5], stats[0:1] + stats[1:2]


def kernel(
    nx, nz, ny,
    lat_hbm, fr_hbm, lists_ref, qw_hbm, kw_hbm, vw_hbm, ow_hbm, out_ref,
    lat, fr, qw, kw, vw, ow, bias, q_all, q_aug, kv_send, kv_recv, k_aug, v_aug,
    top_ref, acc, pa_send, pa_recv, pb_send, pb_recv, fin_send, fin_recv,
    load_sem, zq_s, zq_r, xq_s, xq_r, kv_s, kv_r, pa_s, pa_r, pb_s, pb_r, fin_s, fin_r,
):
    ctx, head = lax.axis_index("ctx"), lax.axis_index("head")
    x, z = ctx // nz, lax.rem(ctx, nz)
    y, c = head // 2, lax.rem(head, 2)
    heads = 2 * ny
    own = lat.shape[0]
    group = nz * own
    total_rows = nx * group
    frames = fr.shape[0]
    keys = 2 * frames
    width = out_ref.shape[1]

    loads = []

    def load(src, dst):
        copy = pltpu.make_async_copy(src, dst, load_sem.at[len(loads)])
        copy.start()
        loads.append(copy)
        return copy

    y_order = far_first(ny) + [0]
    load_lat = load(lat_hbm, lat)
    load_qw = load(qw_hbm, qw)
    load_fr = load(fr_hbm, fr)
    load_kv = []
    for i, step in enumerate(y_order):
        cols = pl.ds(pl.multiple_of(lax.rem(y + step, ny) * 2 * LANES, 2 * LANES), 2 * LANES)
        load_kv.append((load(kw_hbm.at[:, cols], kw.at[i]), load(vw_hbm.at[:, cols], vw.at[i])))
    load_ow = load(ow_hbm, ow)

    barrier = pltpu.get_barrier_semaphore()
    z_steps, x_steps, h_steps = far_first(nz), far_first(nx), range(1, heads)

    def z_peer(step):
        return lax.rem(z + step, nz)

    def x_peer(step):
        return lax.rem(x + step, nx)

    def h_peer(step):
        return lax.rem(head + step, heads)

    for step in z_steps:
        pl.semaphore_signal(barrier, inc=1, device_id=(x * nz + z_peer(step), head), device_id_type=MESH)
    for step in x_steps:
        pl.semaphore_signal(barrier, inc=1, device_id=(x_peer(step) * nz + z, head), device_id_type=MESH)
    for step in h_steps:
        pl.semaphore_signal(barrier, inc=1, device_id=(ctx, h_peer(step)), device_id_type=MESH)

    own_rows = pl.ds(pl.multiple_of(ctx * own, own), own)
    load_lat.wait()
    load_qw.wait()
    q_all[own_rows, :] = jnp.dot(lat[...], qw[...], preferred_element_type=F32).astype(BF16)
    pl.semaphore_wait(barrier, len(z_steps) + len(x_steps) + len(h_steps))

    def remote(src, dst, send, recv, device):
        return pltpu.make_async_remote_copy(
            src_ref=src, dst_ref=dst, send_sem=send, recv_sem=recv, device_id=device, device_id_type=MESH
        )

    sent = []

    def push(*args):
        copy = remote(*args)
        copy.start()
        sent.append(copy)

    for step in z_steps:
        push(q_all.at[own_rows, :], q_all.at[own_rows, :], zq_s.at[step], zq_r.at[z], (x * nz + z_peer(step), head))

    load_fr.wait()
    for i, step in enumerate(y_order):
        for copy in load_kv[i]:
            copy.wait()
        yd = lax.rem(y + step, ny)
        k = jnp.dot(fr[...], kw[i], preferred_element_type=F32).astype(BF16)
        v = jnp.dot(fr[...], vw[i], preferred_element_type=F32).astype(BF16)
        for cd in range(2):
            kv_send[i, cd, 0] = k[:, cd * LANES:(cd + 1) * LANES]
            kv_send[i, cd, 1] = v[:, cd * LANES:(cd + 1) * LANES]
        if step:
            for cd in range(2):
                push(kv_send.at[i, cd], kv_recv.at[y, c], kv_s.at[2 * i + cd], kv_r.at[head], (ctx, 2 * yd + cd))
    push(kv_send.at[ny - 1, 1 - c], kv_recv.at[y, c], kv_s.at[2 * ny - 2], kv_r.at[head], (ctx, 2 * y + 1 - c))
    kv_recv[y, c] = kv_send[ny - 1, c]

    lists = lists_ref[...].astype(F32)
    blocks, listed = lists.shape
    unused = jnp.full((HS - blocks, listed), -1.0, F32)
    lists = jnp.concatenate([lists, unused, lists, unused], axis=0).T
    local_blocks = heads * frames // BLK
    for j in range(local_blocks):
        block_id = (ctx * local_blocks + j).astype(F32)
        seen = jnp.max(jnp.where(lists == block_id, 1.0, 0.0), axis=0, keepdims=True)
        bias[j] = jnp.broadcast_to(jnp.where(seen > 0.0, 0.0, NEG), (8, LANES))

    for step in z_steps:
        zs = z_peer(step)
        rows = pl.ds(pl.multiple_of((x * nz + zs) * own, own), own)
        remote(q_all.at[rows, :], q_all.at[rows, :], zq_s.at[step], zq_r.at[zs], (ctx, head)).wait_recv()

    def group_rows(xg):
        return pl.ds(pl.multiple_of(xg * group, group), group)

    for step in x_steps:
        push(
            q_all.at[group_rows(x), :], q_all.at[group_rows(x), :], xq_s.at[step], xq_r.at[x],
            (x_peer(step) * nz + z, head),
        )

    lane = lax.broadcasted_iota(jnp.int32, (1, LANES), 1)
    low = lane < HS

    def build_queries(xg):
        q = q_all[group_rows(xg), :].astype(F32) * SCALE
        high = q.astype(BF16)
        rest = (q - high.astype(F32)).astype(BF16)
        block = (lax.broadcasted_iota(jnp.int32, (group, 1), 0) + xg * group) // BLK
        own_block = jnp.where(lax.rem(lane, HS) == block, 1.0, 0.0).astype(BF16)
        zero = jnp.zeros_like(high)
        for h in range(2):
            mine = low if h == 0 else ~low
            q_aug[h, group_rows(xg), 0:LANES] = jnp.where(mine, high, own_block)
            q_aug[h, group_rows(xg), LANES:2 * LANES] = jnp.where(mine, rest, zero)

    def build_keys(yk):
        vt = []
        for cs in range(2):
            k = kv_recv[yk, cs, 0]
            for j in range(frames // BLK):
                row = bias[(yk * 2 + cs) * (frames // BLK) + j][0:1].astype(BF16)
                place = slice(cs * frames + j * BLK, cs * frames + (j + 1) * BLK)
                kj = k[j * BLK:(j + 1) * BLK]
                for h in range(2):
                    mine = low if h == 0 else ~low
                    k_aug[h, place, 0:LANES] = jnp.where(mine, kj, jnp.broadcast_to(row, kj.shape))
                    k_aug[h, place, LANES:2 * LANES] = kj
            vt.append(kv_recv[yk, cs, 1].astype(F32).T.astype(BF16))
        vt = jnp.concatenate(vt, axis=1)
        ones = jnp.ones((16, keys), BF16)
        for h in range(2):
            v_aug[h, 0:HS] = vt[h * HS:(h + 1) * HS]
            v_aug[h, HS:PACK] = ones

    def attend(rows, first):
        for h in range(2):
            s = lax.dot_general(
                k_aug[h], q_aug[h, rows, :], (((1,), (1,)), ((), ())), preferred_element_type=F32
            )
            top = jnp.max(s, axis=0, keepdims=True)
            if not first:
                old = top_ref[h, 0:1, rows]
                top = jnp.maximum(top, old)
            p = jnp.exp2(s - top).astype(BF16)
            part = jnp.dot(v_aug[h], p, preferred_element_type=F32)
            if not first:
                part = part + acc[h, :, rows] * jnp.exp2(old - top)
            acc[h, :, rows] = part
            top_ref[h, 0:1, rows] = top

    def wait_keys(yk, cores):
        for cs in cores:
            slot = kv_recv.at[yk, cs]
            remote(slot, slot, kv_s.at[0], kv_r.at[2 * yk + cs], (ctx, head)).wait_recv()

    wait_keys(y, [1 - c])
    build_keys(y)
    for step in near_first(nx):
        xg = x_peer(step)
        if step:
            rows = group_rows(xg)
            remote(q_all.at[rows, :], q_all.at[rows, :], xq_s.at[step], xq_r.at[xg], (ctx, head)).wait_recv()
        build_queries(xg)
        attend(group_rows(xg), True)

    others = near_first(ny)[1:]
    for step in others[:-1]:
        yk = lax.rem(y + step, ny)
        wait_keys(yk, range(2))
        build_keys(yk)
        attend(pl.ds(0, total_rows), False)
    yk = lax.rem(y + others[-1], ny)
    wait_keys(yk, range(2))
    build_keys(yk)
    for step in x_steps + [0]:
        xg = x_peer(step)
        rows = group_rows(xg)
        attend(rows, False)
        if step:
            for h in range(2):
                pa_send[step, h, 0:HS] = acc[h, 0:HS, rows].astype(BF16)
                pa_send[step, h, HS:PACK] = pack_stats(top_ref[h, 0:1, rows], acc[h, HS:HS + 1, rows])
            push(pa_send.at[step], pa_recv.at[x], pa_s.at[step], pa_r.at[x], (xg * nz + z, head))

    for step in x_steps:
        slot = pa_recv.at[x_peer(step)]
        remote(slot, slot, pa_s.at[step], pa_r.at[x_peer(step)], (ctx, head)).wait_recv()
    packed = []
    for h in range(2):
        rows = group_rows(x)
        tops, totals = [top_ref[h, 0:1, rows]], [acc[h, HS:HS + 1, rows]]
        for step in x_steps:
            one_top, one_total = unpack_stats(pa_recv[x_peer(step), h, HS:PACK])
            tops.append(one_top)
            totals.append(one_total)
        top = functools.reduce(jnp.maximum, tops)
        factors = [jnp.exp2(one - top) for one in tops]
        total = sum(one * factor for one, factor in zip(totals, factors))
        value = acc[h, 0:HS, rows] * factors[0]
        for step, factor in zip(x_steps, factors[1:]):
            value = value + pa_recv[x_peer(step), h, 0:HS].astype(F32) * factor
        packed.append((value, pack_stats(top, total).astype(F32)))
    for t in range(group // LANES):
        cols = slice(t * LANES, (t + 1) * LANES)
        for part, place in ((0, slice(0, HS)), (1, slice(HS, PACK))):
            a, b = packed[0][part][:, cols], packed[1][part][:, cols]
            pb_send[2 * t, place] = jnp.where(low, a, pltpu.roll(b, HS, 1)).astype(BF16)
            pb_send[2 * t + 1, place] = jnp.where(low, pltpu.roll(a, HS, 1), b).astype(BF16)
    for step in z_steps:
        push(pb_send.at[z_peer(step)], pb_recv.at[z], pb_s.at[step], pb_r.at[z], (x * nz + z_peer(step), head))
    load_ow.wait()

    messages = [pb_send[z]]
    for step in z_steps:
        slot = pb_recv.at[z_peer(step)]
        remote(slot, slot, pb_s.at[step], pb_r.at[z_peer(step)], (ctx, head)).wait_recv()
        messages.append(pb_recv[z_peer(step)])
    stats = [unpack_stats(message[HS:PACK]) for message in messages]
    top = functools.reduce(jnp.maximum, [one for one, _ in stats])
    factors = [jnp.exp2(one - top) for one, _ in stats]
    total = sum(one * factor for (_, one), factor in zip(stats, factors))
    value = sum(message[0:HS].astype(F32) * factor for message, factor in zip(messages, factors))
    attended = (value / total).T.astype(BF16)
    mixed = jnp.dot(attended[0:own], ow[0:HS], preferred_element_type=F32) + jnp.dot(
        attended[own:2 * own], ow[HS:2 * HS], preferred_element_type=F32
    )

    each = own // heads
    half = width // 2
    for h in range(heads):
        rows = mixed[h * each:(h + 1) * each]
        fin_send[h] = jnp.concatenate([rows[:, :half], rows[:, half:]], axis=0).astype(BF16)
    for step in h_steps:
        hd = h_peer(step)
        push(fin_send.at[hd], fin_recv.at[head], fin_s.at[step], fin_r.at[head], (ctx, hd))
    result = fin_send[head].astype(F32)
    for step in h_steps:
        slot = fin_recv.at[h_peer(step)]
        remote(slot, slot, fin_s.at[step], fin_r.at[h_peer(step)], (ctx, head)).wait_recv()
        result = result + fin_recv[h_peer(step)].astype(F32)
    out_ref[:, 0:half] = result[0:each]
    out_ref[:, half:width] = result[each:2 * each]
    for copy in sent:
        copy.wait_send()


def per_device(nx, nz, ny, latents, frames, block_lists, query_weight, key_weight, value_weight, output_weight):
    own, depth = latents.shape
    count = frames.shape[0]
    width = output_weight.shape[1]
    heads, group = 2 * ny, nz * own
    rows = nx * group
    each = own // heads
    any_space, vmem = pl.BlockSpec(memory_space=pl.ANY), pl.BlockSpec(memory_space=pltpu.VMEM)
    dma = pltpu.SemaphoreType.DMA
    mixed = pl.pallas_call(
        functools.partial(kernel, nx, nz, ny),
        out_shape=jax.ShapeDtypeStruct((each, width), F32),
        in_specs=[any_space, any_space, vmem, any_space, any_space, any_space, any_space],
        out_specs=vmem,
        scratch_shapes=[
            pltpu.VMEM((own, depth), BF16),
            pltpu.VMEM((count, depth), BF16),
            pltpu.VMEM((depth, LANES), BF16),
            pltpu.VMEM((ny, depth, 2 * LANES), BF16),
            pltpu.VMEM((ny, depth, 2 * LANES), BF16),
            pltpu.VMEM((LANES, width), BF16),
            pltpu.VMEM((heads * count // BLK, 8, LANES), F32),
            pltpu.VMEM((rows, LANES), BF16),
            pltpu.VMEM((2, rows, 2 * LANES), BF16),
            pltpu.VMEM((ny, 2, 2, count, LANES), BF16),
            pltpu.VMEM((ny, 2, 2, count, LANES), BF16),
            pltpu.VMEM((2, 2 * count, 2 * LANES), BF16),
            pltpu.VMEM((2, PACK, 2 * count), BF16),
            pltpu.VMEM((2, 8, rows), F32),
            pltpu.VMEM((2, PACK, rows), F32),
            pltpu.VMEM((nx, 2, PACK, group), BF16),
            pltpu.VMEM((nx, 2, PACK, group), BF16),
            pltpu.VMEM((nz, PACK, LANES), BF16),
            pltpu.VMEM((nz, PACK, LANES), BF16),
            pltpu.VMEM((heads, 2 * each, width // 2), BF16),
            pltpu.VMEM((heads, 2 * each, width // 2), BF16),
            dma((4 + 2 * ny,)),
            dma((nz,)), dma((nz,)),
            dma((nx,)), dma((nx,)),
            dma((heads,)), dma((heads,)),
            dma((nx,)), dma((nx,)),
            dma((nz,)), dma((nz,)),
            dma((heads,)), dma((heads,)),
        ],
        compiler_params=pltpu.CompilerParams(
            collective_id=0, has_side_effects=True, vmem_limit_bytes=56 * 2**20
        ),
        name="cross_attention",
    )(latents, frames, block_lists, query_weight, key_weight, value_weight, output_weight)
    return mixed.astype(BF16)


def solution(mesh, nx=4, nz=8, ny=4):
    return jax.shard_map(
        functools.partial(per_device, nx, nz, ny),
        mesh=mesh,
        in_specs=(
            P("ctx", None),
            P(("ctx", "head"), None),
            P(),
            P(None, "head"),
            P(),
            P(),
            P("head", None),
        ),
        out_specs=P(("ctx", "head"), None),
        check_vma=False,
    )
```

```python
import functools

import jax
import jax.numpy as jnp
from jax import lax
from jax.experimental import pallas as pl
from jax.experimental.pallas import tpu as pltpu
from jax.sharding import PartitionSpec as P

HS = 64
BLK = 128
LANES = 2 * HS
PACK = HS + 16
SCALE = HS ** (-0.5) * 1.4426950408889634
NEG = -1e30
MESH = pl.DeviceIdType.MESH
F32, BF16 = jnp.float32, jnp.bfloat16


def near_first(count):
    return sorted(range(count), key=lambda step: (min(step, count - step), step))


def far_first(count):
    return [step for step in near_first(count)[::-1] if step]


def split_parts(value, count):
    parts = []
    for _ in range(count):
        part = value.astype(BF16).astype(F32)
        parts.append(part)
        value = value - part
    return parts


def pack_stats(top, total):
    rows = split_parts(total, 2) + split_parts(top, 3)
    row_id = lax.broadcasted_iota(jnp.int32, (16, top.shape[1]), 0)
    out = jnp.zeros((16, top.shape[1]), F32)
    for index, row in enumerate(rows):
        out = jnp.where(row_id == index, jnp.broadcast_to(row, out.shape), out)
    return out.astype(BF16)


def unpack_stats(stats):
    stats = stats.astype(F32)
    return stats[2:3] + stats[3:4] + stats[4:5], stats[0:1] + stats[1:2]


def kernel(
    nx, nz, ny,
    lat_hbm, fr_hbm, lists_ref, qw_hbm, kw_hbm, vw_hbm, ow_hbm, out_ref,
    lat, fr, qw, kw, vw, ow, bias, q_own, q_recv, q_aug, kv_send, kv_recv, k_aug, v_aug,
    scores_0, scores_1, top_ref, acc, p_send, p_recv, fin_send, fin_recv,
    load_sem, q_s, q_r, kv_s, kv_r, p_s, p_r, fin_s, fin_r,
):
    ctx, head = lax.axis_index("ctx"), lax.axis_index("head")
    x, z = ctx // nz, lax.rem(ctx, nz)
    y, c = head // 2, lax.rem(head, 2)
    heads = 2 * ny
    own = lat.shape[0]
    group = nz * own
    width = out_ref.shape[1]
    quarter = lax.rem(x + y, ny)

    def up(value, step, count):
        return lax.rem(value + step, count)

    def down(value, step, count):
        return lax.rem(value + count - step, count)

    loads = []

    def load(src, dst):
        copy = pltpu.make_async_copy(src, dst, load_sem.at[len(loads)])
        copy.start()
        loads.append(copy)
        return copy

    y_order = far_first(ny) + [0]
    load_lat = load(lat_hbm, lat)
    load_qw = load(qw_hbm, qw)
    load_fr = load(fr_hbm, fr)
    load_kv = []
    for step in y_order:
        cols = pl.ds(pl.multiple_of(up(quarter, step, ny) * 2 * LANES, 2 * LANES), 2 * LANES)
        load_kv.append((load(kw_hbm.at[:, cols], kw.at[step]), load(vw_hbm.at[:, cols], vw.at[step])))
    load_ow = load(ow_hbm, ow)

    def user(dx, dz):
        xt = up(x, dx, nx)
        return (xt * nz + up(z, dz, nz), 2 * down(y, xt, ny) + c)

    def owner(dx, dz):
        return (down(x, dx, nx) * nz + down(z, dz, nz), 2 * quarter + c)

    def other_device(dx, dz, action):
        if dx or dz:
            action()
        else:
            pl.when(x != 0)(action)

    x_order = range(nx)
    z_order = far_first(nz) + [0]
    ways = [(dx, dz) for dx in x_order for dz in z_order]

    barrier = pltpu.get_barrier_semaphore()

    def greet(device):
        pl.semaphore_signal(barrier, inc=1, device_id=device, device_id_type=MESH)

    for dx, dz in ways:
        other_device(dx, dz, lambda: greet(owner(dx, dz)))
    for f in range(2):
        for step in range(1, ny):
            core = c if f == 0 else 1 - c
            greet((ctx, 2 * down(y, step, ny) + core))
            greet((down(x, step, nx) * nz + z, 2 * y + core))
    greet((ctx, 2 * y + 1 - c))

    load_lat.wait()
    load_qw.wait()
    q_own[...] = (jnp.dot(lat[...], qw[...], preferred_element_type=F32) * SCALE).astype(BF16)
    pl.semaphore_wait(barrier, nx * nz + 4 * (ny - 1) + jnp.minimum(x, 1))

    def remote(src, dst, send, recv, device):
        return pltpu.make_async_remote_copy(
            src_ref=src, dst_ref=dst, send_sem=send, recv_sem=recv, device_id=device, device_id_type=MESH
        )

    sent = []

    def push(*args):
        copy = remote(*args)
        copy.start()
        sent.append(copy)

    def q_copy(dx, dz):
        index = dx * nz + dz
        return remote(q_own, q_recv.at[dx, dz], q_s.at[index], q_r.at[index], user(dx, dz))

    for dx, dz in ways:
        other_device(dx, dz, lambda: q_copy(dx, dz).start())

    @pl.when(x == 0)
    def _():
        q_recv[0, 0] = q_own[...]

    load_fr.wait()
    for i, step in enumerate(y_order):
        for copy in load_kv[i]:
            copy.wait()
        for part, weight in ((0, kw), (1, vw)):
            rows = jnp.dot(fr[...], weight[step], preferred_element_type=F32).astype(BF16)
            for block in range(2):
                for cd in range(2):
                    kv_send[step, block, cd, part] = rows[
                        block * BLK:(block + 1) * BLK, cd * LANES:(cd + 1) * LANES
                    ]
        for f in range(2):
            core = c if f == 0 else 1 - c
            for block in range(2):
                index = (step * 2 + block) * 2 + f
                if step:
                    if block == 0:
                        device = (ctx, 2 * up(y, step, ny) + core)
                    else:
                        device = (up(x, step, nx) * nz + z, 2 * y + core)
                elif f:
                    device = (ctx, 2 * y + core)
                else:
                    kv_recv[0, block, 0] = kv_send[0, block, core]
                    continue
                push(
                    kv_send.at[step, block, core], kv_recv.at[step, block, f],
                    kv_s.at[index], kv_r.at[index], device,
                )

    lists = lists_ref[...].astype(F32)
    blocks, listed = lists.shape
    unused = jnp.full((HS - blocks, listed), -1.0, F32)
    lists = jnp.concatenate([lists, unused, lists, unused], axis=0).T
    for step in range(ny):
        for block in range(2):
            for f in range(2):
                core = c if f == 0 else 1 - c
                if block == 0:
                    first = ctx * heads + 2 * down(y, step, ny) + core
                else:
                    first = (down(x, step, nx) * nz + z) * heads + 2 * y + core
                block_id = (first * 2 + block).astype(F32)
                seen = jnp.max(jnp.where(lists == block_id, 1.0, 0.0), axis=0, keepdims=True)
                bias[step, block, f] = jnp.broadcast_to(jnp.where(seen > 0.0, 0.0, NEG), (8, LANES))

    lane = lax.broadcasted_iota(jnp.int32, (1, LANES), 1)
    low = lane < HS

    def build_queries(dx):
        for dz in z_order:
            index = dx * nz + dz
            slot = q_recv.at[dx, dz]
            other_device(
                dx, dz,
                lambda: remote(slot, slot, q_s.at[index], q_r.at[index], (ctx, head)).wait_recv(),
            )
        for dz in range(nz):
            q = q_recv[dx, dz]
            block = (down(x, dx, nx) * nz + down(z, dz, nz)) * own // BLK
            own_block = jnp.where(lax.rem(lane, HS) == block, 1.0, 0.0).astype(BF16)
            own_block = jnp.broadcast_to(own_block, q.shape)
            rows = slice(dx * group + dz * own, dx * group + (dz + 1) * own)
            q_aug[0, rows] = jnp.where(low, q, own_block)
            q_aug[1, rows] = jnp.where(low, own_block, q)

    def build_keys(step):
        for block in range(2):
            for f in range(2):
                index = (step * 2 + block) * 2 + f
                slot = kv_recv.at[step, block, f]
                if step or f:
                    remote(slot, slot, kv_s.at[index], kv_r.at[index], (ctx, head)).wait_recv()
        for block in range(2):
            for f in range(2):
                index = (step * 2 + block) * 2 + f
                place = slice(index * BLK, (index + 1) * BLK)
                k = kv_recv[step, block, f, 0]
                hidden = jnp.broadcast_to(bias[step, block, f][0:1].astype(BF16), k.shape)
                k_aug[0, place] = jnp.where(low, k, hidden)
                k_aug[1, place] = jnp.where(low, hidden, k)
                v = kv_recv[step, block, f, 1].astype(F32).T.astype(BF16)
                for h in range(2):
                    v_aug[h, 0:HS, place] = v[h * HS:(h + 1) * HS]
                    v_aug[h, HS:PACK, place] = jnp.ones((PACK - HS, BLK), BF16)

    def product(keys, queries):
        return lax.dot_general(keys, queries, (((1,), (1,)), ((), ())), preferred_element_type=F32)

    def send_partials(dx, values, tops):
        packed = []
        for value, top in zip(values, tops):
            packed.append((value[0:HS], pack_stats(top, value[HS:HS + 1]).astype(F32)))
        for t in range(group // LANES):
            cols = slice(t * LANES, (t + 1) * LANES)
            for part, place in ((0, slice(0, HS)), (1, slice(HS, PACK))):
                a, b = packed[0][part][:, cols], packed[1][part][:, cols]
                p_send[dx, 2 * t, place] = jnp.where(low, a, pltpu.roll(b, HS, 1)).astype(BF16)
                p_send[dx, 2 * t + 1, place] = jnp.where(low, pltpu.roll(a, HS, 1), b).astype(BF16)
        for dz in z_order:
            other_device(dx, dz, lambda: p_copy(dx, dz).start())
        if dx == 0:

            @pl.when(x == 0)
            def _():
                p_recv[0, 0] = p_send[0, 0]

    def p_copy(dx, dz):
        index = dx * nz + dz
        return remote(p_send.at[dx, dz], p_recv.at[dx, dz], p_s.at[index], p_r.at[index], owner(dx, dz))

    build_queries(0)
    rows = slice(0, group)
    for step in range(ny):
        build_keys(step)
        keys = slice(step * 4 * BLK, (step + 1) * 4 * BLK)
        for h in range(2):
            s = product(k_aug[h, keys], q_aug[h, rows])
            top = jnp.max(s, axis=0, keepdims=True)
            if step:
                old = top_ref[h, 0:1]
                top = jnp.maximum(top, old)
            part = jnp.dot(v_aug[h, :, keys], jnp.exp2(s - top).astype(BF16), preferred_element_type=F32)
            if step:
                part = part + acc[h] * jnp.exp2(old - top)
            acc[h] = part
            top_ref[h, 0:1] = top
    send_partials(0, [acc[0], acc[1]], [top_ref[0, 0:1], top_ref[1, 0:1]])

    for dx in x_order[1:]:
        build_queries(dx)
    units = [(dx, h) for dx in x_order[1:] for h in range(2)]
    buffers = (scores_0, scores_1)

    def score(u):
        dx, h = units[u]
        s = product(k_aug[h], q_aug[h, dx * group:(dx + 1) * group])
        buffers[u % 2][...] = s
        return jnp.max(s, axis=0, keepdims=True)

    top = score(0)
    done = []
    for u, (dx, h) in enumerate(units):
        later = score(u + 1) if u + 1 < len(units) else None
        weights = jnp.exp2(buffers[u % 2][...] - top).astype(BF16)
        done.append((jnp.dot(v_aug[h], weights, preferred_element_type=F32), top))
        if h == 1:
            send_partials(dx, [one for one, _ in done], [one for _, one in done])
            done = []
        top = later

    top = total = value = None
    for dx in x_order:
        for dz in z_order:
            index = dx * nz + dz
            slot = p_recv.at[dx, dz]
            other_device(
                dx, dz,
                lambda: remote(slot, slot, p_s.at[index], p_r.at[index], (ctx, head)).wait_recv(),
            )
        stats = [unpack_stats(p_recv[dx, dz, HS:PACK]) for dz in range(nz)]
        tops = [one for one, _ in stats] + ([] if top is None else [top])
        new_top = functools.reduce(jnp.maximum, tops)
        if top is not None:
            factor = jnp.exp2(top - new_top)
            total, value = total * factor, value * factor
        for dz, (one_top, one_total) in enumerate(stats):
            factor = jnp.exp2(one_top - new_top)
            one_total = one_total * factor
            one_value = p_recv[dx, dz, 0:HS].astype(F32) * factor
            total = one_total if total is None else total + one_total
            value = one_value if value is None else value + one_value
        top = new_top
    load_ow.wait()
    attended = (value / total).T.astype(BF16)
    mixed = jnp.dot(attended[0:own], ow[0:HS], preferred_element_type=F32) + jnp.dot(
        attended[own:2 * own], ow[HS:2 * HS], preferred_element_type=F32
    )

    each = own // heads
    half = width // 2
    for h in range(heads):
        rows = mixed[h * each:(h + 1) * each]
        fin_send[h] = jnp.concatenate([rows[:, :half], rows[:, half:]], axis=0).astype(BF16)
    h_steps = range(1, heads)
    for step in h_steps:
        hd = up(head, step, heads)
        push(fin_send.at[hd], fin_recv.at[step], fin_s.at[step], fin_r.at[step], (ctx, hd))
    result = fin_send[head].astype(F32)
    for step in h_steps:
        slot = fin_recv.at[step]
        remote(slot, slot, fin_s.at[step], fin_r.at[step], (ctx, head)).wait_recv()
        result = result + fin_recv[step].astype(F32)
    out_ref[...] = jnp.concatenate([result[0:each], result[each:2 * each]], axis=1).astype(out_ref.dtype)
    for copy in sent:
        copy.wait_send()
    for dx, dz in ways:
        other_device(dx, dz, lambda: q_copy(dx, dz).wait_send())
        other_device(dx, dz, lambda: p_copy(dx, dz).wait_send())


def per_device(nx, nz, ny, latents, frames, block_lists, query_weight, key_weight, value_weight, output_weight):
    own, depth = latents.shape
    count = frames.shape[0]
    width = output_weight.shape[1]
    heads, group = 2 * ny, nz * own
    rows = nx * group
    keys = ny * 4 * BLK
    each = own // heads
    any_space, vmem = pl.BlockSpec(memory_space=pl.ANY), pl.BlockSpec(memory_space=pltpu.VMEM)
    dma = pltpu.SemaphoreType.DMA
    return pl.pallas_call(
        functools.partial(kernel, nx, nz, ny),
        out_shape=jax.ShapeDtypeStruct((each, width), BF16),
        in_specs=[any_space, any_space, vmem, any_space, any_space, any_space, any_space],
        out_specs=vmem,
        scratch_shapes=[
            pltpu.VMEM((own, depth), BF16),
            pltpu.VMEM((count, depth), BF16),
            pltpu.VMEM((depth, LANES), BF16),
            pltpu.VMEM((ny, depth, 2 * LANES), BF16),
            pltpu.VMEM((ny, depth, 2 * LANES), BF16),
            pltpu.VMEM((LANES, width), BF16),
            pltpu.VMEM((ny, 2, 2, 8, LANES), F32),
            pltpu.VMEM((own, LANES), BF16),
            pltpu.VMEM((nx, nz, own, LANES), BF16),
            pltpu.VMEM((2, rows, LANES), BF16),
            pltpu.VMEM((ny, 2, 2, 2, BLK, LANES), BF16),
            pltpu.VMEM((ny, 2, 2, 2, BLK, LANES), BF16),
            pltpu.VMEM((2, keys, LANES), BF16),
            pltpu.VMEM((2, PACK, keys), BF16),
            pltpu.VMEM((keys, group), F32),
            pltpu.VMEM((keys, group), F32),
            pltpu.VMEM((2, 8, group), F32),
            pltpu.VMEM((2, PACK, group), F32),
            pltpu.VMEM((nx, nz, PACK, LANES), BF16),
            pltpu.VMEM((nx, nz, PACK, LANES), BF16),
            pltpu.VMEM((heads, 2 * each, width // 2), BF16),
            pltpu.VMEM((heads, 2 * each, width // 2), BF16),
            dma((4 + 2 * ny,)),
            dma((nx * nz,)), dma((nx * nz,)),
            dma((4 * ny,)), dma((4 * ny,)),
            dma((nx * nz,)), dma((nx * nz,)),
            dma((heads,)), dma((heads,)),
        ],
        compiler_params=pltpu.CompilerParams(
            collective_id=0, has_side_effects=True, vmem_limit_bytes=56 * 2**20
        ),
        name="cross_attention",
    )(latents, frames, block_lists, query_weight, key_weight, value_weight, output_weight)


def solution(mesh, nx=4, nz=8, ny=4):
    return jax.shard_map(
        functools.partial(per_device, nx, nz, ny),
        mesh=mesh,
        in_specs=(
            P("ctx", None),
            P(("ctx", "head"), None),
            P(),
            P(None, "head"),
            P(),
            P(),
            P("head", None),
        ),
        out_specs=P(("ctx", "head"), None),
        check_vma=False,
    )
```

```python
import functools

import jax
import jax.numpy as jnp
from jax import lax
from jax.experimental import pallas as pl
from jax.experimental.pallas import tpu as pltpu
from jax.sharding import PartitionSpec as P

HS = 64
BLK = 128
LANES = 2 * HS
PACK = HS + 16
SCALE = HS ** (-0.5) * 1.4426950408889634
NEG = -1e30
MESH = pl.DeviceIdType.MESH
F32, BF16 = jnp.float32, jnp.bfloat16


def near_first(count):
    return sorted(range(count), key=lambda step: (min(step, count - step), step))


def far_first(count):
    return [step for step in near_first(count)[::-1] if step]


def split_parts(value, count):
    parts = []
    for _ in range(count):
        part = value.astype(BF16).astype(F32)
        parts.append(part)
        value = value - part
    return parts


def pack_stats(top, total):
    rows = split_parts(total, 2) + split_parts(top, 3)
    row_id = lax.broadcasted_iota(jnp.int32, (16, top.shape[1]), 0)
    out = jnp.zeros((16, top.shape[1]), F32)
    for index, row in enumerate(rows):
        out = jnp.where(row_id == index, jnp.broadcast_to(row, out.shape), out)
    return out.astype(BF16)


def unpack_stats(stats):
    stats = stats.astype(F32)
    return stats[2:3] + stats[3:4] + stats[4:5], stats[0:1] + stats[1:2]


def kernel(
    nx, nz, ny,
    lat_hbm, fr_hbm, lists_hbm, qw_hbm, kw_hbm, vw_hbm, ow_hbm, out_ref,
    lat, fr, lists_ref, qw, kw, vw, ow, bias, q_own, q_recv, q_aug, kv_send, kv_recv, k_aug, v_aug,
    scores_0, scores_1, top_ref, acc, a_send, a_recv, p_send, p_recv, fin_send, fin_recv,
    load_sem, q_s, q_r, qx_s, qx_r, kv_s, kv_r, a_s, a_r, p_s, p_r, fin_s, fin_r,
):
    ctx, head = lax.axis_index("ctx"), lax.axis_index("head")
    x, z = ctx // nz, lax.rem(ctx, nz)
    y, c = head // 2, lax.rem(head, 2)
    heads = 2 * ny
    own = lat.shape[0]
    group = nz * own
    width = out_ref.shape[1]
    quarter = lax.rem(y + z, ny)
    at_home = lax.rem(z, ny) == 0

    def up(value, step, count):
        return lax.rem(value + step, count)

    def down(value, step, count):
        return lax.rem(value + count - step, count)

    loads = []

    def load(src, dst):
        copy = pltpu.make_async_copy(src, dst, load_sem.at[len(loads)])
        copy.start()
        loads.append(copy)
        return copy

    y_order = far_first(ny) + [0]
    load_lat = load(lat_hbm, lat)
    load_qw = load(qw_hbm, qw)
    load_lists = load(lists_hbm, lists_ref)
    load_fr = load(fr_hbm, fr)
    load_kv = []
    for step in y_order:
        cols = pl.ds(pl.multiple_of(up(quarter, step, ny) * 2 * LANES, 2 * LANES), 2 * LANES)
        load_kv.append((load(kw_hbm.at[:, cols], kw.at[step]), load(vw_hbm.at[:, cols], vw.at[step])))
    load_ow = load(ow_hbm, ow)

    def user(dz):
        zt = up(z, dz, nz)
        return (x * nz + zt, 2 * down(y, lax.rem(zt, ny), ny) + c)

    def owner(dz):
        return (x * nz + down(z, dz, nz), 2 * quarter + c)

    def other_device(dz, action):
        if dz:
            action()
        else:
            pl.when(jnp.logical_not(at_home))(action)

    def z_steps(step, core):
        if step in (0, 1):
            return step
        if step == ny - 1:
            return nz - 1
        return step + core * (nz - 2 * step)

    def core_of(f):
        return c if f == 0 else 1 - c

    def frames_to(step, block, f):
        if block == 0:
            return (ctx, 2 * up(y, step, ny) + core_of(f))
        return (x * nz + up(z, z_steps(step, c), nz), 2 * y + core_of(f))

    def frames_from(step, block, f):
        if block == 0:
            return (ctx, 2 * down(y, step, ny) + core_of(f))
        return (x * nz + down(z, z_steps(step, core_of(f)), nz), 2 * y + core_of(f))

    barrier = pltpu.get_barrier_semaphore()

    def greet(device):
        pl.semaphore_signal(barrier, inc=1, device_id=device, device_id_type=MESH)

    z_far, x_far = far_first(nz), far_first(nx)
    for dz in z_far + [0]:
        other_device(dz, lambda: greet(owner(dz)))
    for dx in x_far:
        greet((down(x, dx, nx) * nz + z, head))
    for step in far_first(ny):
        for block in range(2):
            for f in range(2):
                greet(frames_from(step, block, f))
    greet((ctx, 2 * y + 1 - c))

    load_lat.wait()
    load_qw.wait()
    q_own[...] = (jnp.dot(lat[...], qw[...], preferred_element_type=F32) * SCALE).astype(BF16)
    greeted = nz - 1 + nx - 1 + 4 * (ny - 1) + 1
    pl.semaphore_wait(barrier, greeted + jnp.minimum(lax.rem(z, ny), 1))

    def remote(src, dst, send, recv, device):
        return pltpu.make_async_remote_copy(
            src_ref=src, dst_ref=dst, send_sem=send, recv_sem=recv, device_id=device, device_id_type=MESH
        )

    sent = []

    def push(*args):
        copy = remote(*args)
        copy.start()
        sent.append(copy)

    def q_copy(dz):
        return remote(q_own, q_recv.at[0, dz], q_s.at[dz], q_r.at[dz], user(dz))

    for dz in z_far + [0]:
        other_device(dz, lambda: q_copy(dz).start())

    @pl.when(at_home)
    def _():
        q_recv[0, 0] = q_own[...]

    load_lists.wait()
    lists = lists_ref[...].astype(F32)
    blocks, listed = lists.shape
    unused = jnp.full((HS - blocks, listed), -1.0, F32)
    lists = jnp.concatenate([lists, unused, lists, unused], axis=0).T
    for step in range(ny):
        for block in range(2):
            for f in range(2):
                from_ctx, from_head = frames_from(step, block, f)
                block_id = ((from_ctx * heads + from_head) * 2 + block).astype(F32)
                seen = jnp.max(jnp.where(lists == block_id, 1.0, 0.0), axis=0, keepdims=True)
                bias[step, block, f] = jnp.broadcast_to(jnp.where(seen > 0.0, 0.0, NEG), (8, LANES))

    load_fr.wait()
    for i, step in enumerate(y_order):
        for copy in load_kv[i]:
            copy.wait()
        for part, weight in ((0, kw), (1, vw)):
            rows = jnp.dot(fr[...], weight[step], preferred_element_type=F32).astype(BF16)
            for block in range(2):
                for cd in range(2):
                    kv_send[step, block, cd, part] = rows[
                        block * BLK:(block + 1) * BLK, cd * LANES:(cd + 1) * LANES
                    ]
        for f in range(2):
            for block in range(2):
                index = (step * 2 + block) * 2 + f
                if step or f:
                    push(
                        kv_send.at[step, block, core_of(f)], kv_recv.at[step, block, f],
                        kv_s.at[index], kv_r.at[index], frames_to(step, block, f),
                    )
                else:
                    kv_recv[0, block, 0] = kv_send[0, block, c]

    for dz in near_first(nz):
        slot = q_recv.at[0, dz]
        other_device(dz, lambda: remote(slot, slot, q_s.at[dz], q_r.at[dz], (ctx, head)).wait_recv())
        for dx in x_far:
            index = dx * nz + dz
            push(slot, q_recv.at[dx, dz], qx_s.at[index], qx_r.at[index], (up(x, dx, nx) * nz + z, head))

    lane = lax.broadcasted_iota(jnp.int32, (1, LANES), 1)
    low = lane < HS

    def build_queries(dx):
        if dx:
            for dz in range(nz):
                index = dx * nz + dz
                slot = q_recv.at[dx, dz]
                remote(slot, slot, qx_s.at[index], qx_r.at[index], (ctx, head)).wait_recv()
        for dz in range(nz):
            q = q_recv[dx, dz]
            block = (down(x, dx, nx) * nz + down(z, dz, nz)) * own // BLK
            own_block = jnp.where(lax.rem(lane, HS) == block, 1.0, 0.0).astype(BF16)
            own_block = jnp.broadcast_to(own_block, q.shape)
            rows = slice(dx * group + dz * own, dx * group + (dz + 1) * own)
            q_aug[0, rows] = jnp.where(low, q, own_block)
            q_aug[1, rows] = jnp.where(low, own_block, q)

    def build_keys(step):
        for block in range(2):
            for f in range(2):
                index = (step * 2 + block) * 2 + f
                slot = kv_recv.at[step, block, f]
                if step or f:
                    remote(slot, slot, kv_s.at[index], kv_r.at[index], (ctx, head)).wait_recv()
        for block in range(2):
            for f in range(2):
                index = (step * 2 + block) * 2 + f
                place = slice(index * BLK, (index + 1) * BLK)
                k = kv_recv[step, block, f, 0]
                hidden = jnp.broadcast_to(bias[step, block, f][0:1].astype(BF16), k.shape)
                k_aug[0, place] = jnp.where(low, k, hidden)
                k_aug[1, place] = jnp.where(low, hidden, k)
                v = kv_recv[step, block, f, 1].astype(F32).T.astype(BF16)
                for h in range(2):
                    v_aug[h, 0:HS, place] = v[h * HS:(h + 1) * HS]
                    v_aug[h, HS:PACK, place] = jnp.ones((PACK - HS, BLK), BF16)

    def product(keys, queries):
        return lax.dot_general(keys, queries, (((1,), (1,)), ((), ())), preferred_element_type=F32)

    def first_group(step, first):
        build_keys(step)
        keys = slice(step * 4 * BLK, (step + 1) * 4 * BLK)
        for h in range(2):
            s = product(k_aug[h, keys], q_aug[h, 0:group])
            top = jnp.max(s, axis=0, keepdims=True)
            if not first:
                old = top_ref[h, 0:1]
                top = jnp.maximum(top, old)
            part = jnp.dot(v_aug[h, :, keys], jnp.exp2(s - top).astype(BF16), preferred_element_type=F32)
            if not first:
                part = part + acc[h] * jnp.exp2(old - top)
            acc[h] = part
            top_ref[h, 0:1] = top

    build_queries(0)
    for step in near_first(ny):
        first_group(step, step == 0)

    units = [(dx, h) for dx in x_far for h in range(2)]
    buffers = (scores_0, scores_1)

    def score(u):
        dx, h = units[u]
        if h == 0:
            build_queries(dx)
        s = product(k_aug[h], q_aug[h, dx * group:(dx + 1) * group])
        buffers[u % 2][...] = s
        return jnp.max(s, axis=0, keepdims=True)

    top = score(0)
    for u, (dx, h) in enumerate(units):
        later = score(u + 1) if u + 1 < len(units) else None
        weights = jnp.exp2(buffers[u % 2][...] - top).astype(BF16)
        part = jnp.dot(v_aug[h], weights, preferred_element_type=F32)
        a_send[dx, h, 0:HS] = part[0:HS].astype(BF16)
        a_send[dx, h, HS:PACK] = pack_stats(top, part[HS:HS + 1])
        index = 2 * dx + h
        push(
            a_send.at[dx, h], a_recv.at[dx, h], a_s.at[index], a_r.at[index],
            (down(x, dx, nx) * nz + z, head),
        )
        top = later

    packed = []
    for h in range(2):
        tops, totals = [top_ref[h, 0:1]], [acc[h, HS:HS + 1]]
        for dx in x_far:
            index = 2 * dx + h
            slot = a_recv.at[dx, h]
            remote(slot, slot, a_s.at[index], a_r.at[index], (ctx, head)).wait_recv()
            one_top, one_total = unpack_stats(a_recv[dx, h, HS:PACK])
            tops.append(one_top)
            totals.append(one_total)
        top = functools.reduce(jnp.maximum, tops)
        factors = [jnp.exp2(one - top) for one in tops]
        total = sum(one * factor for one, factor in zip(totals, factors))
        value = acc[h, 0:HS] * factors[0]
        for dx, factor in zip(x_far, factors[1:]):
            value = value + a_recv[dx, h, 0:HS].astype(F32) * factor
        packed.append((value, pack_stats(top, total).astype(F32)))
    for t in range(group // LANES):
        cols = slice(t * LANES, (t + 1) * LANES)
        for part, place in ((0, slice(0, HS)), (1, slice(HS, PACK))):
            a, b = packed[0][part][:, cols], packed[1][part][:, cols]
            p_send[2 * t, place] = jnp.where(low, a, pltpu.roll(b, HS, 1)).astype(BF16)
            p_send[2 * t + 1, place] = jnp.where(low, pltpu.roll(a, HS, 1), b).astype(BF16)

    def p_copy(dz):
        return remote(p_send.at[dz], p_recv.at[dz], p_s.at[dz], p_r.at[dz], owner(dz))

    for dz in z_far + [0]:
        other_device(dz, lambda: p_copy(dz).start())

    @pl.when(at_home)
    def _():
        p_recv[0] = p_send[0]

    for dz in z_far + [0]:
        slot = p_recv.at[dz]
        other_device(dz, lambda: remote(slot, slot, p_s.at[dz], p_r.at[dz], (ctx, head)).wait_recv())
    messages = [p_recv[dz] for dz in range(nz)]
    stats = [unpack_stats(message[HS:PACK]) for message in messages]
    top = functools.reduce(jnp.maximum, [one for one, _ in stats])
    factors = [jnp.exp2(one - top) for one, _ in stats]
    total = sum(one * factor for (_, one), factor in zip(stats, factors))
    value = sum(message[0:HS].astype(F32) * factor for message, factor in zip(messages, factors))
    load_ow.wait()
    attended = (value / total).T.astype(BF16)
    mixed = jnp.dot(attended[0:own], ow[0:HS], preferred_element_type=F32) + jnp.dot(
        attended[own:2 * own], ow[HS:2 * HS], preferred_element_type=F32
    )

    each = own // heads
    half = width // 2
    for h in range(heads):
        rows = mixed[h * each:(h + 1) * each]
        fin_send[h] = jnp.concatenate([rows[:, :half], rows[:, half:]], axis=0).astype(BF16)
    h_steps = range(1, heads)
    for step in h_steps:
        hd = up(head, step, heads)
        push(fin_send.at[hd], fin_recv.at[step], fin_s.at[step], fin_r.at[step], (ctx, hd))
    result = fin_send[head].astype(F32)
    for step in h_steps:
        slot = fin_recv.at[step]
        remote(slot, slot, fin_s.at[step], fin_r.at[step], (ctx, head)).wait_recv()
        result = result + fin_recv[step].astype(F32)
    out_ref[...] = jnp.concatenate([result[0:each], result[each:2 * each]], axis=1).astype(out_ref.dtype)
    for copy in sent:
        copy.wait_send()
    for dz in z_far + [0]:
        other_device(dz, lambda: q_copy(dz).wait_send())
        other_device(dz, lambda: p_copy(dz).wait_send())


def per_device(nx, nz, ny, latents, frames, block_lists, query_weight, key_weight, value_weight, output_weight):
    own, depth = latents.shape
    count = frames.shape[0]
    width = output_weight.shape[1]
    heads, group = 2 * ny, nz * own
    rows = nx * group
    keys = ny * 4 * BLK
    each = own // heads
    any_space, vmem = pl.BlockSpec(memory_space=pl.ANY), pl.BlockSpec(memory_space=pltpu.VMEM)
    dma = pltpu.SemaphoreType.DMA
    return pl.pallas_call(
        functools.partial(kernel, nx, nz, ny),
        out_shape=jax.ShapeDtypeStruct((each, width), BF16),
        in_specs=[any_space] * 7,
        out_specs=vmem,
        scratch_shapes=[
            pltpu.VMEM((own, depth), BF16),
            pltpu.VMEM((count, depth), BF16),
            pltpu.VMEM(block_lists.shape, jnp.int32),
            pltpu.VMEM((depth, LANES), BF16),
            pltpu.VMEM((ny, depth, 2 * LANES), BF16),
            pltpu.VMEM((ny, depth, 2 * LANES), BF16),
            pltpu.VMEM((LANES, width), BF16),
            pltpu.VMEM((ny, 2, 2, 8, LANES), F32),
            pltpu.VMEM((own, LANES), BF16),
            pltpu.VMEM((nx, nz, own, LANES), BF16),
            pltpu.VMEM((2, rows, LANES), BF16),
            pltpu.VMEM((ny, 2, 2, 2, BLK, LANES), BF16),
            pltpu.VMEM((ny, 2, 2, 2, BLK, LANES), BF16),
            pltpu.VMEM((2, keys, LANES), BF16),
            pltpu.VMEM((2, PACK, keys), BF16),
            pltpu.VMEM((keys, group), F32),
            pltpu.VMEM((keys, group), F32),
            pltpu.VMEM((2, 8, group), F32),
            pltpu.VMEM((2, PACK, group), F32),
            pltpu.VMEM((nx, 2, PACK, group), BF16),
            pltpu.VMEM((nx, 2, PACK, group), BF16),
            pltpu.VMEM((nz, PACK, LANES), BF16),
            pltpu.VMEM((nz, PACK, LANES), BF16),
            pltpu.VMEM((heads, 2 * each, width // 2), BF16),
            pltpu.VMEM((heads, 2 * each, width // 2), BF16),
            dma((5 + 2 * ny,)),
            dma((nz,)), dma((nz,)),
            dma((nx * nz,)), dma((nx * nz,)),
            dma((4 * ny,)), dma((4 * ny,)),
            dma((2 * nx,)), dma((2 * nx,)),
            dma((nz,)), dma((nz,)),
            dma((heads,)), dma((heads,)),
        ],
        compiler_params=pltpu.CompilerParams(
            collective_id=0, has_side_effects=True, vmem_limit_bytes=56 * 2**20
        ),
        name="cross_attention",
    )(latents, frames, block_lists, query_weight, key_weight, value_weight, output_weight)


def solution(mesh, nx=4, nz=8, ny=4):
    return jax.shard_map(
        functools.partial(per_device, nx, nz, ny),
        mesh=mesh,
        in_specs=(
            P("ctx", None),
            P(("ctx", "head"), None),
            P(),
            P(None, "head"),
            P(),
            P(),
            P("head", None),
        ),
        out_specs=P(("ctx", "head"), None),
        check_vma=False,
    )
```

```python
import functools

import jax
import jax.numpy as jnp
from jax import lax
from jax.experimental import pallas as pl
from jax.experimental.pallas import tpu as pltpu
from jax.sharding import PartitionSpec as P

HS = 64
BLK = 128
LANES = 2 * HS
PACK = HS + 16
HALF = HS // 2
SCALE = HS ** (-0.5) * 1.4426950408889634
NEG = -1e30
MESH = pl.DeviceIdType.MESH
F32, BF16 = jnp.float32, jnp.bfloat16


def near_first(count):
    return sorted(range(count), key=lambda step: (min(step, count - step), step))


def far_first(count):
    return [step for step in near_first(count)[::-1] if step]


def split_parts(value, count):
    parts = []
    for _ in range(count):
        part = value.astype(BF16).astype(F32)
        parts.append(part)
        value = value - part
    return parts


def pack_stats(top, total):
    rows = split_parts(total, 2) + split_parts(top, 3)
    row_id = lax.broadcasted_iota(jnp.int32, (16, top.shape[1]), 0)
    out = jnp.zeros((16, top.shape[1]), F32)
    for index, row in enumerate(rows):
        out = jnp.where(row_id == index, jnp.broadcast_to(row, out.shape), out)
    return out.astype(BF16)


def unpack_stats(stats):
    stats = stats.astype(F32)
    return stats[2:3] + stats[3:4] + stats[4:5], stats[0:1] + stats[1:2]


def kernel(
    nx, nz, ny,
    lat_hbm, fr_hbm, lists_hbm, qw_hbm, kw_hbm, vw_hbm, ow_hbm, out_ref,
    lat, fr, lists_ref, qw, kw, vw, ow, bias, q_own, q_recv, q_aug, kv_send, kv_recv, k_aug, v_aug,
    scores_0, scores_1, top_ref, acc, a_send, a_recv, p_send, p_recv, fin_send, fin_recv,
    load_sem, q_s, q_r, qx_s, qx_r, kv_s, kv_r, a_s, a_r, p_s, p_r, fin_s, fin_r,
):
    ctx, head = lax.axis_index("ctx"), lax.axis_index("head")
    x, z = ctx // nz, lax.rem(ctx, nz)
    y, c = head // 2, lax.rem(head, 2)
    heads = 2 * ny
    own = lat.shape[0]
    group = nz * own
    parts = a_recv.shape[2]
    chunk = group // parts
    width = out_ref.shape[1]
    quarter = lax.rem(y + z, ny)
    at_home = lax.rem(z, ny) == 0

    def up(value, step, count):
        return lax.rem(value + step, count)

    def down(value, step, count):
        return lax.rem(value + count - step, count)

    loads = []

    def load(src, dst):
        copy = pltpu.make_async_copy(src, dst, load_sem.at[len(loads)])
        copy.start()
        loads.append(copy)
        return copy

    y_order = far_first(ny) + [0]
    load_lat = load(lat_hbm, lat)
    load_qw = load(qw_hbm, qw)
    load_lists = load(lists_hbm, lists_ref)
    load_fr = load(fr_hbm, fr)
    load_kv = []
    for step in y_order:
        cols = pl.ds(pl.multiple_of(up(quarter, step, ny) * 2 * LANES, 2 * LANES), 2 * LANES)
        load_kv.append((load(kw_hbm.at[:, cols], kw.at[step]), load(vw_hbm.at[:, cols], vw.at[step])))
    load_ow = load(ow_hbm, ow)

    def user(dz):
        zt = up(z, dz, nz)
        return (x * nz + zt, 2 * down(y, lax.rem(zt, ny), ny) + c)

    def owner(dz):
        return (x * nz + down(z, dz, nz), 2 * quarter + c)

    def other_device(dz, action):
        if dz:
            action()
        else:
            pl.when(jnp.logical_not(at_home))(action)

    def z_steps(step, core):
        if step in (0, 1):
            return step
        if step == ny - 1:
            return nz - 1
        return step + core * (nz - 2 * step)

    def core_of(f):
        return c if f == 0 else 1 - c

    def frames_to(step, block, f):
        if block == 0:
            return (ctx, 2 * up(y, step, ny) + core_of(f))
        return (x * nz + up(z, z_steps(step, c), nz), 2 * y + core_of(f))

    def frames_from(step, block, f):
        if block == 0:
            return (ctx, 2 * down(y, step, ny) + core_of(f))
        return (x * nz + down(z, z_steps(step, core_of(f)), nz), 2 * y + core_of(f))

    barrier = pltpu.get_barrier_semaphore()

    def greet(device):
        pl.semaphore_signal(barrier, inc=1, device_id=device, device_id_type=MESH)

    z_far, x_far = far_first(nz), far_first(nx)
    for dz in z_far + [0]:
        other_device(dz, lambda: greet(owner(dz)))
    for dx in x_far:
        greet((down(x, dx, nx) * nz + z, head))
    for step in far_first(ny):
        for block in range(2):
            for f in range(2):
                greet(frames_from(step, block, f))
    greet((ctx, 2 * y + 1 - c))

    load_lat.wait()
    load_qw.wait()
    q_own[...] = (jnp.dot(lat[...], qw[...], preferred_element_type=F32) * SCALE).astype(BF16)
    greeted = nz - 1 + nx - 1 + 4 * (ny - 1) + 1
    pl.semaphore_wait(barrier, greeted + jnp.minimum(lax.rem(z, ny), 1))

    def remote(src, dst, send, recv, device):
        return pltpu.make_async_remote_copy(
            src_ref=src, dst_ref=dst, send_sem=send, recv_sem=recv, device_id=device, device_id_type=MESH
        )

    sent = []

    def push(*args):
        copy = remote(*args)
        copy.start()
        sent.append(copy)

    def q_copy(dz):
        return remote(q_own, q_recv.at[0, dz], q_s.at[dz], q_r.at[dz], user(dz))

    for dz in z_far + [0]:
        other_device(dz, lambda: q_copy(dz).start())

    @pl.when(at_home)
    def _():
        q_recv[0, 0] = q_own[...]

    load_lists.wait()
    lists = lists_ref[...].astype(F32)
    blocks, listed = lists.shape
    unused = jnp.full((HS - blocks, listed), -1.0, F32)
    lists = jnp.concatenate([lists, unused, lists, unused], axis=0).T
    for step in range(ny):
        for block in range(2):
            for f in range(2):
                from_ctx, from_head = frames_from(step, block, f)
                block_id = ((from_ctx * heads + from_head) * 2 + block).astype(F32)
                seen = jnp.max(jnp.where(lists == block_id, 1.0, 0.0), axis=0, keepdims=True)
                bias[step, block, f] = jnp.broadcast_to(jnp.where(seen > 0.0, 0.0, NEG), (8, LANES))

    load_fr.wait()
    for i, step in enumerate(y_order):
        for copy in load_kv[i]:
            copy.wait()
        for part, weight in ((0, kw), (1, vw)):
            rows = jnp.dot(fr[...], weight[step], preferred_element_type=F32).astype(BF16)
            for block in range(2):
                for cd in range(2):
                    kv_send[step, block, cd, part] = rows[
                        block * BLK:(block + 1) * BLK, cd * LANES:(cd + 1) * LANES
                    ]
        for f in range(2):
            for block in range(2):
                index = (step * 2 + block) * 2 + f
                if step or f:
                    push(
                        kv_send.at[step, block, core_of(f)], kv_recv.at[step, block, f],
                        kv_s.at[index], kv_r.at[index], frames_to(step, block, f),
                    )
                else:
                    kv_recv[0, block, 0] = kv_send[0, block, c]

    for dz in near_first(nz):
        slot = q_recv.at[0, dz]
        other_device(dz, lambda: remote(slot, slot, q_s.at[dz], q_r.at[dz], (ctx, head)).wait_recv())
        for dx in x_far:
            index = dx * nz + dz
            push(slot, q_recv.at[dx, dz], qx_s.at[index], qx_r.at[index], (up(x, dx, nx) * nz + z, head))

    lane = lax.broadcasted_iota(jnp.int32, (1, LANES), 1)
    low = lane < HS

    def build_queries(dx):
        if dx:
            for dz in range(nz):
                index = dx * nz + dz
                slot = q_recv.at[dx, dz]
                remote(slot, slot, qx_s.at[index], qx_r.at[index], (ctx, head)).wait_recv()
        for dz in range(nz):
            q = q_recv[dx, dz]
            block = (down(x, dx, nx) * nz + down(z, dz, nz)) * own // BLK
            own_block = jnp.where(lax.rem(lane, HS) == block, 1.0, 0.0).astype(BF16)
            own_block = jnp.broadcast_to(own_block, q.shape)
            rows = slice(dx * group + dz * own, dx * group + (dz + 1) * own)
            q_aug[0, rows] = jnp.where(low, q, own_block)
            q_aug[1, rows] = jnp.where(low, own_block, q)

    def build_keys(step):
        for block in range(2):
            for f in range(2):
                index = (step * 2 + block) * 2 + f
                slot = kv_recv.at[step, block, f]
                if step or f:
                    remote(slot, slot, kv_s.at[index], kv_r.at[index], (ctx, head)).wait_recv()
        for block in range(2):
            for f in range(2):
                index = (step * 2 + block) * 2 + f
                place = slice(index * BLK, (index + 1) * BLK)
                k = kv_recv[step, block, f, 0]
                hidden = jnp.broadcast_to(bias[step, block, f][0:1].astype(BF16), k.shape)
                k_aug[0, place] = jnp.where(low, k, hidden)
                k_aug[1, place] = jnp.where(low, hidden, k)
                v = kv_recv[step, block, f, 1].astype(F32).T.astype(BF16)
                for h in range(2):
                    v_aug[h, 0:HS, place] = v[h * HS:(h + 1) * HS]
                    v_aug[h, HS:PACK, place] = jnp.ones((PACK - HS, BLK), BF16)

    def product(keys, queries):
        return lax.dot_general(keys, queries, (((1,), (1,)), ((), ())), preferred_element_type=F32)

    def first_group(step, first):
        build_keys(step)
        keys = slice(step * 4 * BLK, (step + 1) * 4 * BLK)
        for h in range(2):
            s = product(k_aug[h, keys], q_aug[h, 0:group])
            top = jnp.max(s, axis=0, keepdims=True)
            if not first:
                old = top_ref[h, 0:1]
                top = jnp.maximum(top, old)
            part = jnp.dot(v_aug[h, :, keys], jnp.exp2(s - top).astype(BF16), preferred_element_type=F32)
            if not first:
                part = part + acc[h] * jnp.exp2(old - top)
            acc[h] = part
            top_ref[h, 0:1] = top

    build_queries(0)
    for step in near_first(ny):
        first_group(step, step == 0)

    units = [(h, dx, part) for h in range(2) for dx in x_far for part in range(parts)]
    buffers = (scores_0, scores_1)
    keys = v_aug.shape[2]
    halves = [slice(0, keys // 2), slice(keys // 2, keys)]

    def scored(u, place):
        h, dx, part = units[u]
        first = dx * group + part * chunk
        s = product(k_aug[h, place], q_aug[h, first:first + chunk])
        buffers[u % 2][place] = s
        return jnp.max(s, axis=0, keepdims=True)

    def weighed(u, place, top):
        weights = jnp.exp2(buffers[u % 2][place] - top).astype(BF16)
        return jnp.dot(v_aug[units[u][0], :, place], weights, preferred_element_type=F32)

    def send_unit(u, top, value):
        h, dx, part = units[u]
        a_send[dx, h, part, 0:HS] = value[0:HS].astype(BF16)
        a_send[dx, h, part, HS:PACK] = pack_stats(top, value[HS:HS + 1])
        index = (dx * 2 + h) * parts + part
        push(
            a_send.at[dx, h, part], a_recv.at[dx, h, part], a_s.at[index], a_r.at[index],
            (down(x, dx, nx) * nz + z, head),
        )

    top = None
    for u in range(-1, len(units)):
        tops, values = [], []
        if u + 1 < len(units):
            h, dx, part = units[u + 1]
            if h == 0 and part == 0:
                build_queries(dx)
        for place in halves:
            if u + 1 < len(units):
                tops.append(scored(u + 1, place))
            if u >= 0:
                values.append(weighed(u, place, top))
        if values:
            send_unit(u, top, values[0] + values[1])
        if tops:
            top = jnp.maximum(tops[0], tops[1])

    def merge_x(h):
        for part in range(parts):
            span = slice(part * chunk, (part + 1) * chunk)
            tops, totals = [top_ref[h, 0:1, span]], [acc[h, HS:HS + 1, span]]
            for dx in x_far:
                index = (dx * 2 + h) * parts + part
                slot = a_recv.at[dx, h, part]
                remote(slot, slot, a_s.at[index], a_r.at[index], (ctx, head)).wait_recv()
                one_top, one_total = unpack_stats(a_recv[dx, h, part, HS:PACK])
                tops.append(one_top)
                totals.append(one_total)
            top = functools.reduce(jnp.maximum, tops)
            factors = [jnp.exp2(one - top) for one in tops]
            total = sum(one * factor for one, factor in zip(totals, factors))
            value = acc[h, 0:HS, span] * factors[0]
            for dx, factor in zip(x_far, factors[1:]):
                value = value + a_recv[dx, h, part, 0:HS].astype(F32) * factor
            stats = pack_stats(top, total).astype(F32)
            for t in range(chunk // LANES):
                cols = slice(t * LANES, (t + 1) * LANES)
                dz = 2 * (part * (chunk // LANES) + t)
                for a, b, place in (
                    (value[0:HALF, cols], value[HALF:HS, cols], slice(0, HALF)),
                    (stats[:, cols], stats[:, cols], slice(HALF, HALF + 16)),
                ):
                    p_send[h, dz, place] = jnp.where(low, a, pltpu.roll(b, HS, 1)).astype(BF16)
                    p_send[h, dz + 1, place] = jnp.where(low, pltpu.roll(a, HS, 1), b).astype(BF16)
        for dz in z_far + [0]:
            other_device(dz, lambda: p_copy(h, dz).start())

        @pl.when(at_home)
        def _():
            p_recv[h, 0] = p_send[h, 0]

    def p_copy(h, dz):
        index = h * nz + dz
        return remote(p_send.at[h, dz], p_recv.at[h, dz], p_s.at[index], p_r.at[index], owner(dz))

    def merge_z(h):
        for dz in z_far + [0]:
            index = h * nz + dz
            slot = p_recv.at[h, dz]
            other_device(
                dz, lambda: remote(slot, slot, p_s.at[index], p_r.at[index], (ctx, head)).wait_recv()
            )
        stats = [unpack_stats(p_recv[h, dz, HALF:HALF + 16]) for dz in range(nz)]
        top = functools.reduce(jnp.maximum, [one for one, _ in stats])
        factors = [jnp.exp2(one - top) for one, _ in stats]
        total = sum(one * factor for (_, one), factor in zip(stats, factors))
        value = sum(p_recv[h, dz, 0:HALF].astype(F32) * factors[dz] for dz in range(nz))
        attended = (value / total).T.astype(BF16)
        return jnp.dot(attended[0:own], ow[h * HS:h * HS + HALF], preferred_element_type=F32) + jnp.dot(
            attended[own:2 * own], ow[h * HS + HALF:(h + 1) * HS], preferred_element_type=F32
        )

    merge_x(0)
    merge_x(1)
    load_ow.wait()
    mixed = merge_z(0)
    mixed = mixed + merge_z(1)

    each = own // heads
    half = width // 2
    for h in range(heads):
        rows = mixed[h * each:(h + 1) * each]
        fin_send[h] = jnp.concatenate([rows[:, :half], rows[:, half:]], axis=0).astype(BF16)
    ways = [(step, f) for step in far_first(ny) + [0] for f in range(2) if step or f]
    for step, f in ways:
        hd = 2 * up(y, step, ny) + core_of(f)
        index = 2 * step + f
        push(fin_send.at[hd], fin_recv.at[index], fin_s.at[index], fin_r.at[index], (ctx, hd))
    result = fin_send[head].astype(F32)
    for step, f in ways[::-1]:
        index = 2 * step + f
        slot = fin_recv.at[index]
        remote(slot, slot, fin_s.at[index], fin_r.at[index], (ctx, head)).wait_recv()
        result = result + fin_recv[index].astype(F32)
    out_ref[...] = jnp.concatenate([result[0:each], result[each:2 * each]], axis=1).astype(out_ref.dtype)
    for copy in sent:
        copy.wait_send()
    for dz in z_far + [0]:
        other_device(dz, lambda: q_copy(dz).wait_send())
        for h in range(2):
            other_device(dz, lambda: p_copy(h, dz).wait_send())


def per_device(nx, nz, ny, latents, frames, block_lists, query_weight, key_weight, value_weight, output_weight):
    own, depth = latents.shape
    count = frames.shape[0]
    width = output_weight.shape[1]
    heads, group = 2 * ny, nz * own
    rows = nx * group
    keys = ny * 4 * BLK
    parts = 2 if group >= 4 * HS else 1
    each = own // heads
    any_space, vmem = pl.BlockSpec(memory_space=pl.ANY), pl.BlockSpec(memory_space=pltpu.VMEM)
    dma = pltpu.SemaphoreType.DMA
    return pl.pallas_call(
        functools.partial(kernel, nx, nz, ny),
        out_shape=jax.ShapeDtypeStruct((each, width), BF16),
        in_specs=[any_space] * 7,
        out_specs=vmem,
        scratch_shapes=[
            pltpu.VMEM((own, depth), BF16),
            pltpu.VMEM((count, depth), BF16),
            pltpu.VMEM(block_lists.shape, jnp.int32),
            pltpu.VMEM((depth, LANES), BF16),
            pltpu.VMEM((ny, depth, 2 * LANES), BF16),
            pltpu.VMEM((ny, depth, 2 * LANES), BF16),
            pltpu.VMEM((LANES, width), BF16),
            pltpu.VMEM((ny, 2, 2, 8, LANES), F32),
            pltpu.VMEM((own, LANES), BF16),
            pltpu.VMEM((nx, nz, own, LANES), BF16),
            pltpu.VMEM((2, rows, LANES), BF16),
            pltpu.VMEM((ny, 2, 2, 2, BLK, LANES), BF16),
            pltpu.VMEM((ny, 2, 2, 2, BLK, LANES), BF16),
            pltpu.VMEM((2, keys, LANES), BF16),
            pltpu.VMEM((2, PACK, keys), BF16),
            pltpu.VMEM((keys, group // parts), F32),
            pltpu.VMEM((keys, group // parts), F32),
            pltpu.VMEM((2, 8, group), F32),
            pltpu.VMEM((2, PACK, group), F32),
            pltpu.VMEM((nx, 2, parts, PACK, group // parts), BF16),
            pltpu.VMEM((nx, 2, parts, PACK, group // parts), BF16),
            pltpu.VMEM((2, nz, HALF + 16, LANES), BF16),
            pltpu.VMEM((2, nz, HALF + 16, LANES), BF16),
            pltpu.VMEM((heads, 2 * each, width // 2), BF16),
            pltpu.VMEM((heads, 2 * each, width // 2), BF16),
            dma((5 + 2 * ny,)),
            dma((nz,)), dma((nz,)),
            dma((nx * nz,)), dma((nx * nz,)),
            dma((4 * ny,)), dma((4 * ny,)),
            dma((2 * nx * parts,)), dma((2 * nx * parts,)),
            dma((2 * nz,)), dma((2 * nz,)),
            dma((heads,)), dma((heads,)),
        ],
        compiler_params=pltpu.CompilerParams(
            collective_id=0, has_side_effects=True, vmem_limit_bytes=56 * 2**20
        ),
        name="cross_attention",
    )(latents, frames, block_lists, query_weight, key_weight, value_weight, output_weight)


def solution(mesh, nx=4, nz=8, ny=4):
    return jax.shard_map(
        functools.partial(per_device, nx, nz, ny),
        mesh=mesh,
        in_specs=(
            P("ctx", None),
            P(("ctx", "head"), None),
            P(),
            P(None, "head"),
            P(),
            P(),
            P("head", None),
        ),
        out_specs=P(("ctx", "head"), None),
        check_vma=False,
    )
```

```python
import functools

import jax
import jax.numpy as jnp
from jax import lax
from jax.experimental import pallas as pl
from jax.experimental.pallas import tpu as pltpu
from jax.sharding import PartitionSpec as P

HS = 64
BLK = 128
LANES = 2 * HS
PACK = HS + 16
HALF = HS // 2
SCALE = HS ** (-0.5) * 1.4426950408889634
NEG = -1e30
MESH = pl.DeviceIdType.MESH
F32, BF16 = jnp.float32, jnp.bfloat16


def near_first(count):
    return sorted(range(count), key=lambda step: (min(step, count - step), step))


def far_first(count):
    return [step for step in near_first(count)[::-1] if step]


def split_parts(value, count):
    parts = []
    for _ in range(count):
        part = value.astype(BF16).astype(F32)
        parts.append(part)
        value = value - part
    return parts


def pack_stats(top, total):
    rows = split_parts(total, 2) + split_parts(top, 3)
    row_id = lax.broadcasted_iota(jnp.int32, (16, top.shape[1]), 0)
    out = jnp.zeros((16, top.shape[1]), F32)
    for index, row in enumerate(rows):
        out = jnp.where(row_id == index, jnp.broadcast_to(row, out.shape), out)
    return out.astype(BF16)


def unpack_stats(stats):
    stats = stats.astype(F32)
    return stats[2:3] + stats[3:4] + stats[4:5], stats[0:1] + stats[1:2]


def kernel(
    nx, nz, ny,
    lat_hbm, fr_hbm, lists_hbm, qw_hbm, kw_hbm, vw_hbm, ow_hbm, out_ref,
    lat, fr, lists_ref, qw, kw, vw, ow, bias, q_own, q_recv, q_aug, kv_send, kv_recv, k_aug, v_aug,
    scores_0, scores_1, top_ref, acc, a_send, a_recv, p_send, p_recv, fin_send, fin_recv,
    load_sem, q_s, q_r, qx_s, qx_r, kv_s, kv_r, a_s, a_r, p_s, p_r, fin_s, fin_r,
):
    ctx, head = lax.axis_index("ctx"), lax.axis_index("head")
    x, z = ctx // nz, lax.rem(ctx, nz)
    y, c = head // 2, lax.rem(head, 2)
    heads = 2 * ny
    own = lat.shape[0]
    group = nz * own
    parts = a_recv.shape[2]
    chunk = group // parts
    width = out_ref.shape[1]
    quarter = lax.rem(y + z, ny)
    at_home = lax.rem(z, ny) == 0

    def up(value, step, count):
        return lax.rem(value + step, count)

    def down(value, step, count):
        return lax.rem(value + count - step, count)

    def user(dz):
        zt = up(z, dz, nz)
        return (x * nz + zt, 2 * down(y, lax.rem(zt, ny), ny) + c)

    def owner(dz):
        return (x * nz + down(z, dz, nz), 2 * quarter + c)

    def other_device(dz, action):
        if dz:
            action()
        else:
            pl.when(jnp.logical_not(at_home))(action)

    def z_steps(step, core):
        if step in (0, 1):
            return step
        if step == ny - 1:
            return nz - 1
        return step + core * (nz - 2 * step)

    def core_of(f):
        return c if f == 0 else 1 - c

    def frames_to(step, block, f):
        if block == 0:
            return (ctx, 2 * up(y, step, ny) + core_of(f))
        return (x * nz + up(z, z_steps(step, c), nz), 2 * y + core_of(f))

    def frames_from(step, block, f):
        if block == 0:
            return (ctx, 2 * down(y, step, ny) + core_of(f))
        return (x * nz + down(z, z_steps(step, core_of(f)), nz), 2 * y + core_of(f))

    barrier = pltpu.get_barrier_semaphore()

    def greet(device):
        pl.semaphore_signal(barrier, inc=1, device_id=device, device_id_type=MESH)

    z_far, x_far = far_first(nz), far_first(nx)
    for dz in z_far + [0]:
        other_device(dz, lambda: greet(owner(dz)))
    for dx in x_far:
        greet((down(x, dx, nx) * nz + z, head))
    for step in far_first(ny):
        for block in range(2):
            for f in range(2):
                greet(frames_from(step, block, f))
    greet((ctx, 2 * y + 1 - c))

    loads = []

    def load(src, dst):
        copy = pltpu.make_async_copy(src, dst, load_sem.at[len(loads)])
        copy.start()
        loads.append(copy)
        return copy

    y_order = far_first(ny) + [0]
    load_lat = load(lat_hbm, lat)
    load_qw = load(qw_hbm, qw)
    load_lists = load(lists_hbm, lists_ref)
    load_fr = load(fr_hbm, fr)
    load_kv = []
    for step in y_order:
        cols = pl.ds(pl.multiple_of(up(quarter, step, ny) * 2 * LANES, 2 * LANES), 2 * LANES)
        load_kv.append((load(kw_hbm.at[:, cols], kw.at[step]), load(vw_hbm.at[:, cols], vw.at[step])))
    load_ow = load(ow_hbm, ow)

    load_lat.wait()
    load_qw.wait()
    q_own[...] = (jnp.dot(lat[...], qw[...], preferred_element_type=F32) * SCALE).astype(BF16)
    def project_frames(i):
        step = y_order[i]
        for copy in load_kv[i]:
            copy.wait()
        for part, weight in ((0, kw), (1, vw)):
            rows = jnp.dot(fr[...], weight[step], preferred_element_type=F32).astype(BF16)
            for block in range(2):
                for cd in range(2):
                    kv_send[step, block, cd, part] = rows[
                        block * BLK:(block + 1) * BLK, cd * LANES:(cd + 1) * LANES
                    ]

    load_fr.wait()
    project_frames(0)
    greeted = nz - 1 + nx - 1 + 4 * (ny - 1) + 1
    pl.semaphore_wait(barrier, greeted + jnp.minimum(lax.rem(z, ny), 1))

    def remote(src, dst, send, recv, device):
        return pltpu.make_async_remote_copy(
            src_ref=src, dst_ref=dst, send_sem=send, recv_sem=recv, device_id=device, device_id_type=MESH
        )

    sent = []

    def push(*args):
        copy = remote(*args)
        copy.start()
        sent.append(copy)

    def q_copy(dz):
        return remote(q_own, q_recv.at[0, dz], q_s.at[dz], q_r.at[dz], user(dz))

    for dz in z_far + [0]:
        other_device(dz, lambda: q_copy(dz).start())

    @pl.when(at_home)
    def _():
        q_recv[0, 0] = q_own[...]

    load_lists.wait()
    lists = lists_ref[...].astype(F32)
    blocks, listed = lists.shape
    unused = jnp.full((HS - blocks, listed), -1.0, F32)
    lists = jnp.concatenate([lists, unused, lists, unused], axis=0).T
    for step in range(ny):
        for block in range(2):
            for f in range(2):
                from_ctx, from_head = frames_from(step, block, f)
                block_id = ((from_ctx * heads + from_head) * 2 + block).astype(F32)
                seen = jnp.max(jnp.where(lists == block_id, 1.0, 0.0), axis=0, keepdims=True)
                bias[step, block, f] = jnp.broadcast_to(jnp.where(seen > 0.0, 0.0, NEG), (8, LANES))

    for i, step in enumerate(y_order):
        if i:
            project_frames(i)
        for f in range(2):
            for block in range(2):
                index = (step * 2 + block) * 2 + f
                if step or f:
                    push(
                        kv_send.at[step, block, core_of(f)], kv_recv.at[step, block, f],
                        kv_s.at[index], kv_r.at[index], frames_to(step, block, f),
                    )
                else:
                    kv_recv[0, block, 0] = kv_send[0, block, c]

    for dz in near_first(nz):
        slot = q_recv.at[0, dz]
        other_device(dz, lambda: remote(slot, slot, q_s.at[dz], q_r.at[dz], (ctx, head)).wait_recv())
        for dx in x_far:
            index = dx * nz + dz
            push(slot, q_recv.at[dx, dz], qx_s.at[index], qx_r.at[index], (up(x, dx, nx) * nz + z, head))

    lane = lax.broadcasted_iota(jnp.int32, (1, LANES), 1)
    low = lane < HS

    def build_queries(dx):
        if dx:
            for dz in range(nz):
                index = dx * nz + dz
                slot = q_recv.at[dx, dz]
                remote(slot, slot, qx_s.at[index], qx_r.at[index], (ctx, head)).wait_recv()
        for dz in range(nz):
            q = q_recv[dx, dz]
            block = (down(x, dx, nx) * nz + down(z, dz, nz)) * own // BLK
            own_block = jnp.where(lax.rem(lane, HS) == block, 1.0, 0.0).astype(BF16)
            own_block = jnp.broadcast_to(own_block, q.shape)
            rows = slice(dx * group + dz * own, dx * group + (dz + 1) * own)
            q_aug[0, rows] = jnp.where(low, q, own_block)
            q_aug[1, rows] = jnp.where(low, own_block, q)

    def build_keys(step):
        for block in range(2):
            for f in range(2):
                index = (step * 2 + block) * 2 + f
                slot = kv_recv.at[step, block, f]
                if step or f:
                    remote(slot, slot, kv_s.at[index], kv_r.at[index], (ctx, head)).wait_recv()
        for block in range(2):
            for f in range(2):
                index = (step * 2 + block) * 2 + f
                place = slice(index * BLK, (index + 1) * BLK)
                k = kv_recv[step, block, f, 0]
                hidden = jnp.broadcast_to(bias[step, block, f][0:1].astype(BF16), k.shape)
                k_aug[0, place] = jnp.where(low, k, hidden)
                k_aug[1, place] = jnp.where(low, hidden, k)
                v = kv_recv[step, block, f, 1].astype(F32).T.astype(BF16)
                for h in range(2):
                    v_aug[h, 0:HS, place] = v[h * HS:(h + 1) * HS]
                    v_aug[h, HS:PACK, place] = jnp.ones((PACK - HS, BLK), BF16)

    def product(keys, queries):
        return lax.dot_general(keys, queries, (((1,), (1,)), ((), ())), preferred_element_type=F32)

    build_queries(0)
    for step in near_first(ny):
        build_keys(step)

    units = [(h, dx, part) for h in range(2) for dx in x_far for part in range(parts)]
    units += [(h, 0, part) for h in range(2) for part in range(parts)]
    buffers = (scores_0, scores_1)
    keys = v_aug.shape[2]
    halves = [slice(0, keys // 2), slice(keys // 2, keys)]

    def scored(u, place):
        h, dx, part = units[u]
        first = dx * group + part * chunk
        s = product(k_aug[h, place], q_aug[h, first:first + chunk])
        buffers[u % 2][place] = s
        return jnp.max(s, axis=0, keepdims=True)

    def weighed(u, place, top):
        weights = jnp.exp2(buffers[u % 2][place] - top).astype(BF16)
        return jnp.dot(v_aug[units[u][0], :, place], weights, preferred_element_type=F32)

    def finish_unit(u, top, value):
        h, dx, part = units[u]
        if dx == 0:
            span = slice(part * chunk, (part + 1) * chunk)
            acc[h, :, span] = value
            top_ref[h, 0:1, span] = top
            return
        a_send[dx, h, part, 0:HS] = value[0:HS].astype(BF16)
        a_send[dx, h, part, HS:PACK] = pack_stats(top, value[HS:HS + 1])
        index = (dx * 2 + h) * parts + part
        push(
            a_send.at[dx, h, part], a_recv.at[dx, h, part], a_s.at[index], a_r.at[index],
            (down(x, dx, nx) * nz + z, head),
        )

    def merge_x(h):
        for part in range(parts):
            span = slice(part * chunk, (part + 1) * chunk)
            tops, totals = [top_ref[h, 0:1, span]], [acc[h, HS:HS + 1, span]]
            for dx in x_far:
                index = (dx * 2 + h) * parts + part
                slot = a_recv.at[dx, h, part]
                remote(slot, slot, a_s.at[index], a_r.at[index], (ctx, head)).wait_recv()
                one_top, one_total = unpack_stats(a_recv[dx, h, part, HS:PACK])
                tops.append(one_top)
                totals.append(one_total)
            top = functools.reduce(jnp.maximum, tops)
            factors = [jnp.exp2(one - top) for one in tops]
            total = sum(one * factor for one, factor in zip(totals, factors))
            value = acc[h, 0:HS, span] * factors[0]
            for dx, factor in zip(x_far, factors[1:]):
                value = value + a_recv[dx, h, part, 0:HS].astype(F32) * factor
            stats = pack_stats(top, total).astype(F32)
            for t in range(chunk // LANES):
                cols = slice(t * LANES, (t + 1) * LANES)
                dz = 2 * (part * (chunk // LANES) + t)
                for a, b, place in (
                    (value[0:HALF, cols], value[HALF:HS, cols], slice(0, HALF)),
                    (stats[:, cols], stats[:, cols], slice(HALF, HALF + 16)),
                ):
                    p_send[h, dz, place] = jnp.where(low, a, pltpu.roll(b, HS, 1)).astype(BF16)
                    p_send[h, dz + 1, place] = jnp.where(low, pltpu.roll(a, HS, 1), b).astype(BF16)
        for dz in z_far + [0]:
            other_device(dz, lambda: p_copy(h, dz).start())

        @pl.when(at_home)
        def _():
            p_recv[h, 0] = p_send[h, 0]

    def p_copy(h, dz):
        index = h * nz + dz
        return remote(p_send.at[h, dz], p_recv.at[h, dz], p_s.at[index], p_r.at[index], owner(dz))

    def merge_z(h):
        for dz in z_far + [0]:
            index = h * nz + dz
            slot = p_recv.at[h, dz]
            other_device(
                dz, lambda: remote(slot, slot, p_s.at[index], p_r.at[index], (ctx, head)).wait_recv()
            )
        stats = [unpack_stats(p_recv[h, dz, HALF:HALF + 16]) for dz in range(nz)]
        top = functools.reduce(jnp.maximum, [one for one, _ in stats])
        factors = [jnp.exp2(one - top) for one, _ in stats]
        total = sum(one * factor for (_, one), factor in zip(stats, factors))
        value = sum(p_recv[h, dz, 0:HALF].astype(F32) * factors[dz] for dz in range(nz))
        attended = (value / total).T.astype(BF16)
        return jnp.dot(attended[0:own], ow[h * HS:h * HS + HALF], preferred_element_type=F32) + jnp.dot(
            attended[own:2 * own], ow[h * HS + HALF:(h + 1) * HS], preferred_element_type=F32
        )

    top = None
    for u in range(-1, len(units)):
        tops, values = [], []
        if u + 1 < len(units):
            h, dx, part = units[u + 1]
            if h == 0 and part == 0 and dx:
                build_queries(dx)
        for place in halves:
            if u + 1 < len(units):
                tops.append(scored(u + 1, place))
            if u >= 0:
                values.append(weighed(u, place, top))
        if values:
            finish_unit(u, top, values[0] + values[1])
            if units[u] == (0, 0, parts - 1):
                merge_x(0)
        if tops:
            top = jnp.maximum(tops[0], tops[1])

    merge_x(1)
    load_ow.wait()
    mixed = merge_z(0)
    mixed = mixed + merge_z(1)

    each = own // heads
    half = width // 2
    for h in range(heads):
        rows = mixed[h * each:(h + 1) * each]
        fin_send[h] = jnp.concatenate([rows[:, :half], rows[:, half:]], axis=0).astype(BF16)
    ways = [(step, f) for step in far_first(ny) + [0] for f in range(2) if step or f]
    for step, f in ways:
        hd = 2 * up(y, step, ny) + core_of(f)
        index = 2 * step + f
        push(fin_send.at[hd], fin_recv.at[index], fin_s.at[index], fin_r.at[index], (ctx, hd))
    result = fin_send[head].astype(F32)
    for step, f in ways[::-1]:
        index = 2 * step + f
        slot = fin_recv.at[index]
        remote(slot, slot, fin_s.at[index], fin_r.at[index], (ctx, head)).wait_recv()
        result = result + fin_recv[index].astype(F32)
    out_ref[...] = jnp.concatenate([result[0:each], result[each:2 * each]], axis=1).astype(out_ref.dtype)
    for copy in sent:
        copy.wait_send()
    for dz in z_far + [0]:
        other_device(dz, lambda: q_copy(dz).wait_send())
        for h in range(2):
            other_device(dz, lambda: p_copy(h, dz).wait_send())


def per_device(nx, nz, ny, latents, frames, block_lists, query_weight, key_weight, value_weight, output_weight):
    own, depth = latents.shape
    count = frames.shape[0]
    width = output_weight.shape[1]
    heads, group = 2 * ny, nz * own
    rows = nx * group
    keys = ny * 4 * BLK
    parts = 2 if group >= 4 * HS else 1
    each = own // heads
    any_space, vmem = pl.BlockSpec(memory_space=pl.ANY), pl.BlockSpec(memory_space=pltpu.VMEM)
    dma = pltpu.SemaphoreType.DMA
    return pl.pallas_call(
        functools.partial(kernel, nx, nz, ny),
        out_shape=jax.ShapeDtypeStruct((each, width), BF16),
        in_specs=[any_space] * 7,
        out_specs=vmem,
        scratch_shapes=[
            pltpu.VMEM((own, depth), BF16),
            pltpu.VMEM((count, depth), BF16),
            pltpu.VMEM(block_lists.shape, jnp.int32),
            pltpu.VMEM((depth, LANES), BF16),
            pltpu.VMEM((ny, depth, 2 * LANES), BF16),
            pltpu.VMEM((ny, depth, 2 * LANES), BF16),
            pltpu.VMEM((LANES, width), BF16),
            pltpu.VMEM((ny, 2, 2, 8, LANES), F32),
            pltpu.VMEM((own, LANES), BF16),
            pltpu.VMEM((nx, nz, own, LANES), BF16),
            pltpu.VMEM((2, rows, LANES), BF16),
            pltpu.VMEM((ny, 2, 2, 2, BLK, LANES), BF16),
            pltpu.VMEM((ny, 2, 2, 2, BLK, LANES), BF16),
            pltpu.VMEM((2, keys, LANES), BF16),
            pltpu.VMEM((2, PACK, keys), BF16),
            pltpu.VMEM((keys, group // parts), F32),
            pltpu.VMEM((keys, group // parts), F32),
            pltpu.VMEM((2, 8, group), F32),
            pltpu.VMEM((2, PACK, group), F32),
            pltpu.VMEM((nx, 2, parts, PACK, group // parts), BF16),
            pltpu.VMEM((nx, 2, parts, PACK, group // parts), BF16),
            pltpu.VMEM((2, nz, HALF + 16, LANES), BF16),
            pltpu.VMEM((2, nz, HALF + 16, LANES), BF16),
            pltpu.VMEM((heads, 2 * each, width // 2), BF16),
            pltpu.VMEM((heads, 2 * each, width // 2), BF16),
            dma((5 + 2 * ny,)),
            dma((nz,)), dma((nz,)),
            dma((nx * nz,)), dma((nx * nz,)),
            dma((4 * ny,)), dma((4 * ny,)),
            dma((2 * nx * parts,)), dma((2 * nx * parts,)),
            dma((2 * nz,)), dma((2 * nz,)),
            dma((heads,)), dma((heads,)),
        ],
        compiler_params=pltpu.CompilerParams(
            collective_id=0, has_side_effects=True, vmem_limit_bytes=56 * 2**20
        ),
        name="cross_attention",
    )(latents, frames, block_lists, query_weight, key_weight, value_weight, output_weight)


def solution(mesh, nx=4, nz=8, ny=4):
    return jax.shard_map(
        functools.partial(per_device, nx, nz, ny),
        mesh=mesh,
        in_specs=(
            P("ctx", None),
            P(("ctx", "head"), None),
            P(),
            P(None, "head"),
            P(),
            P(),
            P("head", None),
        ),
        out_specs=P(("ctx", "head"), None),
        check_vma=False,
    )
```

```python
import functools

import jax
import jax.numpy as jnp
from jax import lax
from jax.experimental import pallas as pl
from jax.experimental.pallas import tpu as pltpu
from jax.sharding import PartitionSpec as P

HS = 64
BLK = 128
LANES = 2 * HS
PACK = HS + 16
HALF = HS // 2
SCALE = HS ** (-0.5) * 1.4426950408889634
NEG = -1e30
MESH = pl.DeviceIdType.MESH
F32, BF16 = jnp.float32, jnp.bfloat16


def near_first(count):
    return sorted(range(count), key=lambda step: (min(step, count - step), step))


def far_first(count):
    return [step for step in near_first(count)[::-1] if step]


def split_parts(value, count):
    parts = []
    for _ in range(count):
        part = value.astype(BF16).astype(F32)
        parts.append(part)
        value = value - part
    return parts


def pack_stats(top, total):
    rows = split_parts(total, 2) + split_parts(top, 3)
    row_id = lax.broadcasted_iota(jnp.int32, (16, top.shape[1]), 0)
    out = jnp.zeros((16, top.shape[1]), F32)
    for index, row in enumerate(rows):
        out = jnp.where(row_id == index, jnp.broadcast_to(row, out.shape), out)
    return out.astype(BF16)


def unpack_stats(stats):
    stats = stats.astype(F32)
    return stats[2:3] + stats[3:4] + stats[4:5], stats[0:1] + stats[1:2]


def kernel(
    nx, nz, ny,
    lat_hbm, fr_hbm, lists_hbm, qw_hbm, kw_hbm, vw_hbm, ow_hbm, out_ref,
    lat, fr, lists_ref, qw, kw, vw, ow, bias, q_own, q_recv, q_aug, kv_send, kv_recv, k_aug, v_aug,
    scores_0, scores_1, top_ref, acc, a_send, a_recv, p_send, p_recv, fin_send, fin_recv,
    load_sem, q_s, q_r, qx_s, qx_r, kv_s, kv_r, a_s, a_r, p_s, p_r, fin_s, fin_r,
):
    ctx, head = lax.axis_index("ctx"), lax.axis_index("head")
    x, z = ctx // nz, lax.rem(ctx, nz)
    y, c = head // 2, lax.rem(head, 2)
    heads = 2 * ny
    own = lat.shape[0]
    group = nz * own
    parts = a_recv.shape[2]
    chunk = group // parts
    width = out_ref.shape[1]
    quarter = lax.rem(y + z, ny)
    at_home = lax.rem(z, ny) == 0

    def up(value, step, count):
        return lax.rem(value + step, count)

    def down(value, step, count):
        return lax.rem(value + count - step, count)

    def user(dz):
        zt = up(z, dz, nz)
        return (x * nz + zt, 2 * down(y, lax.rem(zt, ny), ny) + c)

    def owner(dz):
        return (x * nz + down(z, dz, nz), 2 * quarter + c)

    def other_device(dz, action):
        if dz:
            action()
        else:
            pl.when(jnp.logical_not(at_home))(action)

    def z_steps(step, core):
        if step in (0, 1):
            return step
        if step == ny - 1:
            return nz - 1
        return step + core * (nz - 2 * step)

    def core_of(f):
        return c if f == 0 else 1 - c

    def frames_to(step, block, f):
        if block == 0:
            return (ctx, 2 * up(y, step, ny) + core_of(f))
        return (x * nz + up(z, z_steps(step, c), nz), 2 * y + core_of(f))

    def frames_from(step, block, f):
        if block == 0:
            return (ctx, 2 * down(y, step, ny) + core_of(f))
        return (x * nz + down(z, z_steps(step, core_of(f)), nz), 2 * y + core_of(f))

    barrier = pltpu.get_barrier_semaphore()

    def greet(device):
        pl.semaphore_signal(barrier, inc=1, device_id=device, device_id_type=MESH)

    z_far, x_far = far_first(nz), far_first(nx)
    for dz in z_far + [0]:
        other_device(dz, lambda: greet(owner(dz)))
    for dx in x_far:
        greet((down(x, dx, nx) * nz + z, head))
    for step in far_first(ny):
        for block in range(2):
            for f in range(2):
                greet(frames_from(step, block, f))
    greet((ctx, 2 * y + 1 - c))

    loads = []

    def load(src, dst):
        copy = pltpu.make_async_copy(src, dst, load_sem.at[len(loads)])
        copy.start()
        loads.append(copy)
        return copy

    y_order = far_first(ny) + [0]
    load_lat = load(lat_hbm, lat)
    load_qw = load(qw_hbm, qw)
    load_lists = load(lists_hbm, lists_ref)
    load_fr = load(fr_hbm, fr)
    load_kv = []
    for step in y_order:
        cols = pl.ds(pl.multiple_of(up(quarter, step, ny) * 2 * LANES, 2 * LANES), 2 * LANES)
        load_kv.append((load(kw_hbm.at[:, cols], kw.at[step]), load(vw_hbm.at[:, cols], vw.at[step])))
    load_ow = load(ow_hbm, ow)

    load_lat.wait()
    load_qw.wait()
    q_own[...] = (jnp.dot(lat[...], qw[...], preferred_element_type=F32) * SCALE).astype(BF16)
    def project_frames(i):
        step = y_order[i]
        for copy in load_kv[i]:
            copy.wait()
        for part, weight in ((0, kw), (1, vw)):
            rows = jnp.dot(fr[...], weight[step], preferred_element_type=F32).astype(BF16)
            for block in range(2):
                for cd in range(2):
                    kv_send[step, block, cd, part] = rows[
                        block * BLK:(block + 1) * BLK, cd * LANES:(cd + 1) * LANES
                    ]

    load_fr.wait()
    project_frames(0)
    greeted = nz - 1 + nx - 1 + 4 * (ny - 1) + 1
    pl.semaphore_wait(barrier, greeted + jnp.minimum(lax.rem(z, ny), 1))

    def remote(src, dst, send, recv, device):
        return pltpu.make_async_remote_copy(
            src_ref=src, dst_ref=dst, send_sem=send, recv_sem=recv, device_id=device, device_id_type=MESH
        )

    sent = []

    def push(*args):
        copy = remote(*args)
        copy.start()
        sent.append(copy)

    def q_copy(dz):
        return remote(q_own, q_recv.at[0, dz], q_s.at[dz], q_r.at[dz], user(dz))

    for dz in z_far + [0]:
        other_device(dz, lambda: q_copy(dz).start())

    @pl.when(at_home)
    def _():
        q_recv[0, 0] = q_own[...]

    for i, step in enumerate(y_order):
        if i:
            project_frames(i)
        for f in range(2):
            for block in range(2):
                index = (step * 2 + block) * 2 + f
                if step or f:
                    push(
                        kv_send.at[step, block, core_of(f)], kv_recv.at[step, block, f],
                        kv_s.at[index], kv_r.at[index], frames_to(step, block, f),
                    )
                else:
                    kv_recv[0, block, 0] = kv_send[0, block, c]

    for dz in near_first(nz):
        slot = q_recv.at[0, dz]
        other_device(dz, lambda: remote(slot, slot, q_s.at[dz], q_r.at[dz], (ctx, head)).wait_recv())
        for dx in x_far:
            index = dx * nz + dz
            push(slot, q_recv.at[dx, dz], qx_s.at[index], qx_r.at[index], (up(x, dx, nx) * nz + z, head))

    load_lists.wait()
    lists = lists_ref[...].astype(F32)
    blocks, listed = lists.shape
    unused = jnp.full((HS - blocks, listed), -1.0, F32)
    lists = jnp.concatenate([lists, unused, lists, unused], axis=0).T
    for step in range(ny):
        for block in range(2):
            for f in range(2):
                from_ctx, from_head = frames_from(step, block, f)
                block_id = ((from_ctx * heads + from_head) * 2 + block).astype(F32)
                seen = jnp.max(jnp.where(lists == block_id, 1.0, 0.0), axis=0, keepdims=True)
                bias[step, block, f] = jnp.broadcast_to(jnp.where(seen > 0.0, 0.0, NEG), (8, LANES))

    lane = lax.broadcasted_iota(jnp.int32, (1, LANES), 1)
    low = lane < HS

    def build_queries(dx):
        if dx:
            for dz in range(nz):
                index = dx * nz + dz
                slot = q_recv.at[dx, dz]
                remote(slot, slot, qx_s.at[index], qx_r.at[index], (ctx, head)).wait_recv()
        for dz in range(nz):
            q = q_recv[dx, dz]
            block = (down(x, dx, nx) * nz + down(z, dz, nz)) * own // BLK
            own_block = jnp.where(lax.rem(lane, HS) == block, 1.0, 0.0).astype(BF16)
            own_block = jnp.broadcast_to(own_block, q.shape)
            rows = slice(dx * group + dz * own, dx * group + (dz + 1) * own)
            q_aug[0, rows] = jnp.where(low, q, own_block)
            q_aug[1, rows] = jnp.where(low, own_block, q)

    def build_keys(step):
        for block in range(2):
            for f in range(2):
                index = (step * 2 + block) * 2 + f
                slot = kv_recv.at[step, block, f]
                if step or f:
                    remote(slot, slot, kv_s.at[index], kv_r.at[index], (ctx, head)).wait_recv()
        for block in range(2):
            for f in range(2):
                index = (step * 2 + block) * 2 + f
                place = slice(index * BLK, (index + 1) * BLK)
                k = kv_recv[step, block, f, 0]
                hidden = jnp.broadcast_to(bias[step, block, f][0:1].astype(BF16), k.shape)
                k_aug[0, place] = jnp.where(low, k, hidden)
                k_aug[1, place] = jnp.where(low, hidden, k)
                v = kv_recv[step, block, f, 1].astype(F32).T.astype(BF16)
                for h in range(2):
                    v_aug[h, 0:HS, place] = v[h * HS:(h + 1) * HS]
                    v_aug[h, HS:PACK, place] = jnp.ones((PACK - HS, BLK), BF16)

    def product(keys, queries):
        return lax.dot_general(keys, queries, (((1,), (1,)), ((), ())), preferred_element_type=F32)

    build_queries(0)
    for step in near_first(ny):
        build_keys(step)

    units = [(h, dx, part) for h in range(2) for dx in x_far for part in range(parts)]
    units += [(h, 0, part) for h in range(2) for part in range(parts)]
    buffers = (scores_0, scores_1)
    keys = v_aug.shape[2]
    halves = [slice(0, keys // 2), slice(keys // 2, keys)]

    def scored(u, place):
        h, dx, part = units[u]
        first = dx * group + part * chunk
        s = product(k_aug[h, place], q_aug[h, first:first + chunk])
        buffers[u % 2][place] = s
        return jnp.max(s, axis=0, keepdims=True)

    def weighed(u, place, top):
        weights = jnp.exp2(buffers[u % 2][place] - top).astype(BF16)
        return jnp.dot(v_aug[units[u][0], :, place], weights, preferred_element_type=F32)

    def finish_unit(u, top, value):
        h, dx, part = units[u]
        if dx == 0:
            span = slice(part * chunk, (part + 1) * chunk)
            acc[h, :, span] = value
            top_ref[h, 0:1, span] = top
            return
        a_send[dx, h, part, 0:HS] = value[0:HS].astype(BF16)
        a_send[dx, h, part, HS:PACK] = pack_stats(top, value[HS:HS + 1])
        index = (dx * 2 + h) * parts + part
        push(
            a_send.at[dx, h, part], a_recv.at[dx, h, part], a_s.at[index], a_r.at[index],
            (down(x, dx, nx) * nz + z, head),
        )

    def merge_x(h):
        for part in range(parts):
            span = slice(part * chunk, (part + 1) * chunk)
            tops, totals = [top_ref[h, 0:1, span]], [acc[h, HS:HS + 1, span]]
            for dx in x_far:
                index = (dx * 2 + h) * parts + part
                slot = a_recv.at[dx, h, part]
                remote(slot, slot, a_s.at[index], a_r.at[index], (ctx, head)).wait_recv()
                one_top, one_total = unpack_stats(a_recv[dx, h, part, HS:PACK])
                tops.append(one_top)
                totals.append(one_total)
            top = functools.reduce(jnp.maximum, tops)
            factors = [jnp.exp2(one - top) for one in tops]
            total = sum(one * factor for one, factor in zip(totals, factors))
            value = acc[h, 0:HS, span] * factors[0]
            for dx, factor in zip(x_far, factors[1:]):
                value = value + a_recv[dx, h, part, 0:HS].astype(F32) * factor
            stats = pack_stats(top, total).astype(F32)
            for t in range(chunk // LANES):
                cols = slice(t * LANES, (t + 1) * LANES)
                dz = 2 * (part * (chunk // LANES) + t)
                for a, b, place in (
                    (value[0:HALF, cols], value[HALF:HS, cols], slice(0, HALF)),
                    (stats[:, cols], stats[:, cols], slice(HALF, HALF + 16)),
                ):
                    p_send[h, dz, place] = jnp.where(low, a, pltpu.roll(b, HS, 1)).astype(BF16)
                    p_send[h, dz + 1, place] = jnp.where(low, pltpu.roll(a, HS, 1), b).astype(BF16)
        for dz in z_far + [0]:
            other_device(dz, lambda: p_copy(h, dz).start())

        @pl.when(at_home)
        def _():
            p_recv[h, 0] = p_send[h, 0]

    def p_copy(h, dz):
        index = h * nz + dz
        return remote(p_send.at[h, dz], p_recv.at[h, dz], p_s.at[index], p_r.at[index], owner(dz))

    def merge_z(h):
        for dz in z_far + [0]:
            index = h * nz + dz
            slot = p_recv.at[h, dz]
            other_device(
                dz, lambda: remote(slot, slot, p_s.at[index], p_r.at[index], (ctx, head)).wait_recv()
            )
        stats = [unpack_stats(p_recv[h, dz, HALF:HALF + 16]) for dz in range(nz)]
        top = functools.reduce(jnp.maximum, [one for one, _ in stats])
        factors = [jnp.exp2(one - top) for one, _ in stats]
        total = sum(one * factor for (_, one), factor in zip(stats, factors))
        value = sum(p_recv[h, dz, 0:HALF].astype(F32) * factors[dz] for dz in range(nz))
        attended = (value / total).T.astype(BF16)
        return jnp.dot(attended[0:own], ow[h * HS:h * HS + HALF], preferred_element_type=F32) + jnp.dot(
            attended[own:2 * own], ow[h * HS + HALF:(h + 1) * HS], preferred_element_type=F32
        )

    top = None
    for u in range(-1, len(units)):
        tops, values = [], []
        if u + 1 < len(units):
            h, dx, part = units[u + 1]
            if h == 0 and part == 0 and dx:
                build_queries(dx)
        for place in halves:
            if u + 1 < len(units):
                tops.append(scored(u + 1, place))
            if u >= 0:
                values.append(weighed(u, place, top))
        if values:
            finish_unit(u, top, values[0] + values[1])
            if units[u] == (0, 0, parts - 1):
                merge_x(0)
        if tops:
            top = jnp.maximum(tops[0], tops[1])

    merge_x(1)
    load_ow.wait()
    mixed = merge_z(0)
    mixed = mixed + merge_z(1)

    each = own // heads
    half = width // 2
    for h in range(heads):
        rows = mixed[h * each:(h + 1) * each]
        fin_send[h] = jnp.concatenate([rows[:, :half], rows[:, half:]], axis=0).astype(BF16)
    ways = [(step, f) for step in far_first(ny) + [0] for f in range(2) if step or f]
    for step, f in ways:
        hd = 2 * up(y, step, ny) + core_of(f)
        index = 2 * step + f
        push(fin_send.at[hd], fin_recv.at[index], fin_s.at[index], fin_r.at[index], (ctx, hd))
    result = fin_send[head].astype(F32)
    for step, f in ways[::-1]:
        index = 2 * step + f
        slot = fin_recv.at[index]
        remote(slot, slot, fin_s.at[index], fin_r.at[index], (ctx, head)).wait_recv()
        result = result + fin_recv[index].astype(F32)
    out_ref[...] = jnp.concatenate([result[0:each], result[each:2 * each]], axis=1).astype(out_ref.dtype)
    for copy in sent:
        copy.wait_send()
    for dz in z_far + [0]:
        other_device(dz, lambda: q_copy(dz).wait_send())
        for h in range(2):
            other_device(dz, lambda: p_copy(h, dz).wait_send())


def per_device(nx, nz, ny, latents, frames, block_lists, query_weight, key_weight, value_weight, output_weight):
    own, depth = latents.shape
    count = frames.shape[0]
    width = output_weight.shape[1]
    heads, group = 2 * ny, nz * own
    rows = nx * group
    keys = ny * 4 * BLK
    parts = 1
    each = own // heads
    any_space, vmem = pl.BlockSpec(memory_space=pl.ANY), pl.BlockSpec(memory_space=pltpu.VMEM)
    dma = pltpu.SemaphoreType.DMA
    return pl.pallas_call(
        functools.partial(kernel, nx, nz, ny),
        out_shape=jax.ShapeDtypeStruct((each, width), BF16),
        in_specs=[any_space] * 7,
        out_specs=vmem,
        scratch_shapes=[
            pltpu.VMEM((own, depth), BF16),
            pltpu.VMEM((count, depth), BF16),
            pltpu.VMEM(block_lists.shape, jnp.int32),
            pltpu.VMEM((depth, LANES), BF16),
            pltpu.VMEM((ny, depth, 2 * LANES), BF16),
            pltpu.VMEM((ny, depth, 2 * LANES), BF16),
            pltpu.VMEM((LANES, width), BF16),
            pltpu.VMEM((ny, 2, 2, 8, LANES), F32),
            pltpu.VMEM((own, LANES), BF16),
            pltpu.VMEM((nx, nz, own, LANES), BF16),
            pltpu.VMEM((2, rows, LANES), BF16),
            pltpu.VMEM((ny, 2, 2, 2, BLK, LANES), BF16),
            pltpu.VMEM((ny, 2, 2, 2, BLK, LANES), BF16),
            pltpu.VMEM((2, keys, LANES), BF16),
            pltpu.VMEM((2, PACK, keys), BF16),
            pltpu.VMEM((keys, group // parts), F32),
            pltpu.VMEM((keys, group // parts), F32),
            pltpu.VMEM((2, 8, group), F32),
            pltpu.VMEM((2, PACK, group), F32),
            pltpu.VMEM((nx, 2, parts, PACK, group // parts), BF16),
            pltpu.VMEM((nx, 2, parts, PACK, group // parts), BF16),
            pltpu.VMEM((2, nz, HALF + 16, LANES), BF16),
            pltpu.VMEM((2, nz, HALF + 16, LANES), BF16),
            pltpu.VMEM((heads, 2 * each, width // 2), BF16),
            pltpu.VMEM((heads, 2 * each, width // 2), BF16),
            dma((5 + 2 * ny,)),
            dma((nz,)), dma((nz,)),
            dma((nx * nz,)), dma((nx * nz,)),
            dma((4 * ny,)), dma((4 * ny,)),
            dma((2 * nx * parts,)), dma((2 * nx * parts,)),
            dma((2 * nz,)), dma((2 * nz,)),
            dma((heads,)), dma((heads,)),
        ],
        compiler_params=pltpu.CompilerParams(
            collective_id=0, has_side_effects=True, vmem_limit_bytes=56 * 2**20
        ),
        name="cross_attention",
    )(latents, frames, block_lists, query_weight, key_weight, value_weight, output_weight)


def solution(mesh, nx=4, nz=8, ny=4):
    return jax.shard_map(
        functools.partial(per_device, nx, nz, ny),
        mesh=mesh,
        in_specs=(
            P("ctx", None),
            P(("ctx", "head"), None),
            P(),
            P(None, "head"),
            P(),
            P(),
            P("head", None),
        ),
        out_specs=P(("ctx", "head"), None),
        check_vma=False,
    )
```
